256 devices in a mesh: section: 8 (over x, core), expert: 32 (over y, z).
Axes of the slice: x: 4, y: 4, z: 8, core: 2. Of those that a mesh axis runs over, the one named last changes fastest.
Arguments:
- hidden: bfloat16 [8, 2048, 7168], P('section', 'expert'), may hold values from -6 to 6
- norm_gain: float32 [8, 7168], P('section'), may hold values from 0.5 to 1.5
- gate_weight: bfloat16 [8, 7168, 8192], P('section', None, 'expert'), may hold values from -0.0625 to 0.0625
- up_weight: bfloat16 [8, 7168, 8192], P('section', None, 'expert'), may hold values from -0.0625 to 0.0625
- down_weight: bfloat16 [8, 8192, 7168], P('section', 'expert'), may hold values from -0.1875 to 0.1875
- routes: int32 [8, 2048, 2], P('section', 'expert'), may hold values from 0 to 7, all different within a row; in each aligned block of 64 rows (0 to 63, 64 to 127, ..., all dimensions but the last counted through in order) at most 32 rows name the same one
- logits: float32 [8, 2048, 2], P('section', 'expert'), may hold values from -8 to 8
Outputs:
- mixed: bfloat16 [8, 2048, 7168], P('section', 'expert')
The draws below stay inside these ranges and needn't reach their ends.
Inputs may be any that keep to these rules, and one draw needn't show every extreme that they name: `routes`: each token names 2 different experts. Among the 64 tokens of one device, no expert is named more than 32 times; in every draw the tokens of some device name some expert exactly 32 times.
All inputs are finite; a program needn't handle non-finite values.
Results may differ from the reference program's by a relative error of at most 0.0061.
Values may be sent and summed in bfloat16 or wider, within the bound.
No kernel may reach another device: no remote copies, remote signals or barrier semaphores. Data moves between devices by JAX's collectives and lax.ppermute only.
A program may use at most 192 MiB of HBM per device.

```python
import math
import jax
import jax.numpy as jnp
import numpy as np
from jax import lax

D = 7168
FF = 1024
TOP = 2
TOK_DEV = 64
SECTIONS = 8
EXPERTS = 8
TOKENS = 2048
MOST = 32
N_EXPERT = 32


def block_levels(stream_key, shape, shards, smallest, largest):
    def one(dim, shards_of):
        draws = jax.random.uniform(jax.random.fold_in(jax.random.fold_in(stream_key, 6), dim), (shards_of,), jnp.float32, smallest / len(shards), largest / len(shards))
        return jnp.repeat(jnp.exp(draws), shape[dim] // shards_of).reshape((-1,) + (1,) * (len(shape) - dim - 1))

    factor_of = one(*shards[0])
    for cut in shards[1:]:
        factor_of = factor_of * one(*cut)
    return factor_of


def deal_out(rng, own, number, rows, count, top, most, skew):
    ranking = jax.random.permutation(rng, count)
    packed, common = portions_of(count, rows * top, most, skew, True), portions_of(count, rows * top, most, skew, False)
    places = jnp.arange(count)

    def named(tallies, turn):
        used = int((tallies > 0).sum())
        fixed = max(1, used // 4)
        passed = fixed + (places - fixed + turn * (used - fixed)) % max(1, count - fixed)
        return jnp.zeros((count,), jnp.int32).at[ranking[jnp.where(places < fixed, places, passed)]].set(jnp.asarray(tallies, jnp.int32))

    tallies = jnp.where(number % 4 == 0, named(packed, number // 4), named(common, number - number // 4 - 1))
    mixed = jax.random.permutation(jax.random.fold_in(own, 3), count)
    donor, receiver = mixed[0:count // 2 * 2:2], mixed[1:count // 2 * 2:2]
    room = jnp.minimum(tallies[donor] - 1, most - tallies[receiver]) // 2
    room = jnp.where((donor == ranking[0]) | (receiver == ranking[0]) | (tallies[receiver] == 0), 0, jnp.maximum(room, 0))
    passed = jax.random.randint(jax.random.fold_in(own, 4), (count // 2,), 0, 1 << 20) % (room + 1)
    tallies = tallies.at[donor].add(-passed).at[receiver].add(passed)
    items = jnp.searchsorted(jnp.cumsum(tallies), jnp.arange(rows * top), side="right").astype(jnp.int32)
    table = items.reshape(top, rows).T
    table = table[jax.random.permutation(jax.random.fold_in(own, 1), rows)]
    turn = jax.random.randint(jax.random.fold_in(own, 2), (rows, 1), 0, top)
    return jnp.take_along_axis(table, (jnp.arange(top)[None, :] + turn) % top, axis=1)


def portions_of(amount, total, most, slope, full):
    loads = [(1 << 20) // math.isqrt(standing ** slope) + 1 for standing in range(1, amount + 1)]
    largest = most if full else min(most, max(-(-total // amount), total * loads[0] // sum(loads)))
    least = 1 if total - largest >= amount - 1 else 0
    holding, rest = [largest] + [least] * (amount - 1), total - largest - least * (amount - 1)
    while rest > 0:
        free = [i for i in range(1, amount) if holding[i] < largest] or [i for i in range(1, amount) if holding[i] < most]
        mass, left = sum([loads[i] for i in free]), rest
        for i in free:
            more = min(most - holding[i], max(1, left * loads[i] // mass), rest)
            holding[i] = holding[i] + more
            rest = rest - more
    return np.array(holding)


def scatter_about(stream_key, shape, spread, limit, shards=(), kind=jnp.bfloat16):
    values = jax.random.normal(stream_key, shape, jnp.float32) * spread
    if len(shards) > 0:
        values = block_levels(stream_key, shape, shards, -0.22, 0.18) * values
    return jnp.clip(values, min=-limit, max=limit).astype(kind)


def setup_inputs(seed: int = 0) -> dict:
    key_list = jax.random.split(jax.random.key(seed), 8)
    hidden = scatter_about(key_list[0], (SECTIONS, TOKENS, D), 1.0, 6.0, ((0, 8), (1, 32)))
    norm_gain = jnp.clip(1.0 + 0.1 * jax.random.normal(key_list[1], (SECTIONS, D), jnp.float32), 0.5, 1.5)
    gate_weight = scatter_about(key_list[2], (SECTIONS, D, EXPERTS * FF), D ** -0.5, 0.0625, ((0, 8), (2, 32)))
    up_weight = scatter_about(key_list[3], (SECTIONS, D, EXPERTS * FF), D ** -0.5, 0.0625, ((0, 8), (2, 32)))
    down_weight = scatter_about(key_list[4], (SECTIONS, EXPERTS * FF, D), FF ** -0.5, 0.1875, ((0, 8), (1, 32)))
    routes_keys = jax.random.split(jax.random.fold_in(key_list[5], 1), SECTIONS * TOKENS // TOK_DEV)
    routes_turns = jax.random.permutation(jax.random.fold_in(key_list[5], 3), SECTIONS * TOKENS // TOK_DEV)
    routes = jax.vmap(lambda own, number: deal_out(jax.random.fold_in(key_list[5], 2), own, number, TOK_DEV, EXPERTS, TOP, MOST, 2))(routes_keys, routes_turns).reshape((SECTIONS, TOKENS, TOP))
    logits = scatter_about(key_list[6], (SECTIONS, TOKENS, TOP), 2.0, 8.0, ((0, 8), (1, 32)), jnp.float32)
    return {"hidden": hidden, "norm_gain": norm_gain, "gate_weight": gate_weight, "up_weight": up_weight, "down_weight": down_weight, "routes": routes, "logits": logits}


ROUTE_SCALE = 2.5
EPSILON = 1e-06

def rms_normed(values, gain_row):
    widened = values.astype(jnp.float32)
    scaled = lax.rsqrt(lax.optimization_barrier(jnp.mean(widened * widened, axis=-1, keepdims=True)) + EPSILON)
    return (widened * scaled * gain_row).astype(jnp.bfloat16)

def route_weights(scores):
    gate_values = jax.nn.sigmoid(scores)
    return ROUTE_SCALE * gate_values / lax.optimization_barrier(jnp.sum(gate_values, axis=-1, keepdims=True))

def layer_output(arrived, gain_row, w_gate, w_up, w_down, chosen, scores):
    normed = rms_normed(arrived, gain_row)
    weights = route_weights(scores).reshape(-1)
    flat_routes = chosen.reshape(-1).astype(jnp.int32)
    owner_rows = (jnp.arange(TOKENS * TOP, dtype=jnp.int32) // TOP).astype(jnp.int32)
    capacity = N_EXPERT * MOST

    def per_expert(expert_index):
        order_pairs = jnp.argsort((flat_routes != expert_index).astype(jnp.int32), stable=True)[:capacity].astype(jnp.int32)
        is_valid = (flat_routes[order_pairs] == expert_index).astype(jnp.float32)
        pair_rows = normed[owner_rows[order_pairs]]
        first_col = (expert_index * FF).astype(jnp.int32)
        gate_cols = lax.dynamic_slice_in_dim(w_gate, first_col, FF, 1)
        up_cols = lax.dynamic_slice_in_dim(w_up, first_col, FF, 1)
        down_rows = lax.dynamic_slice_in_dim(w_down, first_col, FF, 0)
        gate_proj = jnp.dot(pair_rows, gate_cols, preferred_element_type=jnp.float32)
        up_proj = jnp.dot(pair_rows, up_cols, preferred_element_type=jnp.float32)
        activated = (jax.nn.silu(gate_proj) * up_proj).astype(jnp.bfloat16)
        expert_output = jnp.dot(activated, down_rows, preferred_element_type=jnp.float32).astype(jnp.bfloat16)
        expert_output = lax.optimization_barrier(expert_output).astype(jnp.float32)
        return (owner_rows[order_pairs], expert_output * (weights[order_pairs] * is_valid)[:, None])
    targets, contributions = lax.map(per_expert, jnp.arange(EXPERTS, dtype=jnp.int32))
    routed_sum = jnp.zeros((TOKENS, D), jnp.float32).at[targets.reshape(-1)].add(contributions.reshape(-1, D))
    return (arrived.astype(jnp.float32) + routed_sum).astype(jnp.bfloat16)

def reference(hidden, norm_gain, gate_weight, up_weight, down_weight, routes, logits):
    arrived = jnp.roll(hidden, 1, axis=0)
    results = [layer_output(arrived[section_index], norm_gain[section_index], gate_weight[section_index], up_weight[section_index], down_weight[section_index], routes[section_index], logits[section_index]) for section_index in range(SECTIONS)]
    return jnp.stack(results)
```

```python
import jax
import jax.numpy as jnp
from jax import lax
from jax.sharding import PartitionSpec as P

ROUTE_SCALE = 2.5
EPSILON = 1e-06
NY = 4
NZ = 8


def moved(x, dy, dz):
    pairs = []
    for y in range(NY):
        for z in range(NZ):
            pairs.append((y * NZ + z, ((y + dy) % NY) * NZ + (z + dz) % NZ))
    return lax.ppermute(x, "expert", pairs)


def next_section(x):
    size = lax.axis_size("section")
    return lax.ppermute(x, "section", [(i, (i + 1) % size) for i in range(size)])


def rms_normed(values, gain_row):
    widened = values.astype(jnp.float32)
    scaled = lax.rsqrt(jnp.mean(widened * widened, axis=-1, keepdims=True) + EPSILON)
    return (widened * scaled * gain_row).astype(jnp.bfloat16)


def route_weights(scores):
    gate_values = jax.nn.sigmoid(scores)
    return ROUTE_SCALE * gate_values / jnp.sum(gate_values, axis=-1, keepdims=True)


def dot(a, b):
    return jnp.dot(a, b, preferred_element_type=jnp.float32)


def across_y(x):
    return moved(x, 2, 0)


def per_device(hidden, norm_gain, gate_weight, up_weight, down_weight, routes, logits):
    bf16 = jnp.bfloat16
    me = lax.axis_index("expert")
    y, z = me // NZ, me % NZ
    tokens, width = hidden.shape[1], hidden.shape[2]
    hid = gate_weight.shape[2]
    part = width // NY
    half = part // 2
    experts = lax.axis_size("expert") // 4

    def w_in(weight):
        def rows_for(d):
            return lax.dynamic_slice(weight, (((y + d) % NY) * part, 0), (part, hid))

        return [
            rows_for(0),
            moved(rows_for(3), -1, 0),
            across_y(rows_for(2)),
            moved(rows_for(1), 1, 0),
        ]

    def w_out(weight):
        def cols_for(d):
            return lax.dynamic_slice(weight, (0, ((y + d) % NY) * part), (hid, part))

        return [
            cols_for(0),
            moved(cols_for(3), -1, 0),
            across_y(cols_for(2)),
            moved(cols_for(1), 1, 0),
        ]

    gates = w_in(gate_weight[0])
    ups = w_in(up_weight[0])
    w_gu = [jnp.concatenate([g, u], axis=1) for g, u in zip(gates, ups)]
    w_down = jnp.concatenate(w_out(down_weight[0]), axis=0)

    chosen = (routes[0][:, :, None] == jnp.arange(experts, dtype=jnp.int32)).astype(jnp.float32)
    table = jnp.sum(chosen * route_weights(logits[0])[:, :, None], axis=1)
    table = lax.all_gather(table, "expert", axis=0, tiled=True)
    mine = (jnp.arange(experts) == me // 4).astype(jnp.float32)
    table = jnp.sum(table * mine, axis=1).reshape(NY, NZ, tokens).transpose(1, 0, 2)
    table = jnp.roll(table, -z, axis=0).reshape(NZ, NY * tokens)

    arrived = next_section(hidden[0])
    normed = rms_normed(arrived, norm_gain[0])

    def quarter(d):
        return lax.dynamic_slice(normed, (0, ((y + d) % NY) * part), (tokens, part))

    block = jnp.stack(
        [quarter(0), moved(quarter(3), -1, 0), across_y(quarter(2)), moved(quarter(1), 1, 0)]
    )
    block = jnp.roll(block, y, axis=0).reshape(NY * tokens, part)
    x = {0: block}
    for k in (1, 2, 3):
        x[k] = moved(x[k - 1], 0, -1)
        x[-k] = moved(x[1 - k], 0, 1)
    x[4] = jnp.concatenate(
        [moved(x[3][:, :half], 0, -1), moved(x[-3][:, half:], 0, 1)], axis=1
    )

    def activated(keys):
        rows = [x[k] for k in keys]
        rows = rows[0] if len(rows) == 1 else jnp.concatenate(rows, axis=0)
        weight = jnp.concatenate([table[k % NZ] for k in keys])[:, None]
        far = dot(rows, w_gu[2]).astype(bf16)
        far_up = moved(far[:, :hid], 1, 0)
        far_down = moved(far[:, hid:], -1, 0)
        right = dot(rows, w_gu[1])
        right = right + jnp.pad(far_up.astype(jnp.float32), ((0, 0), (0, hid)))
        left = dot(rows, w_gu[3])
        left = left + jnp.pad(far_down.astype(jnp.float32), ((0, 0), (hid, 0)))
        right = moved(right.astype(bf16), 1, 0).astype(jnp.float32)
        left = moved(left.astype(bf16), -1, 0).astype(jnp.float32)
        total = dot(rows, w_gu[0]) + right + left
        gate, up = total[:, :hid], total[:, hid:]
        act = (jax.nn.silu(gate) * up * weight).astype(bf16)
        acts = jnp.concatenate(
            [act, moved(act, -1, 0), across_y(act), moved(act, 1, 0)], axis=1
        )
        size = NY * tokens
        return {k: acts[i * size : (i + 1) * size] for i, k in enumerate(keys)}

    acts = {}
    for keys in ((4,), (3, -3), (2, -2), (1, -1), (0,)):
        acts.update(activated(keys))

    wide = [w_down[:, :half], w_down[:, half:]]

    def partial(k, c):
        return dot(acts[k], wide[c])

    def homeward(c, sign, steps):
        sent = None
        for k in range(steps, 0, -1):
            term = partial(4 if k == 4 else sign * k, c)
            if sent is not None:
                term = term + sent.astype(jnp.float32)
            sent = moved(term.astype(bf16), 0, sign)
        return sent.astype(jnp.float32)

    sums = []
    for c in (0, 1):
        plus = homeward(c, 1, 4 if c == 0 else 3)
        minus = homeward(c, -1, 3 if c == 0 else 4)
        sums.append((partial(0, c) + plus + minus).astype(bf16))
    sums = jnp.concatenate(sums, axis=1).reshape(NY, tokens, part)

    def rows_for(d):
        return lax.dynamic_index_in_dim(sums, (y + d) % NY, 0, keepdims=False)

    home = jnp.stack(
        [rows_for(0), moved(rows_for(3), -1, 0), across_y(rows_for(2)), moved(rows_for(1), 1, 0)]
    )
    home = jnp.roll(home, y, axis=0).transpose(1, 0, 2).reshape(tokens, width)
    mixed = (arrived.astype(jnp.float32) + home.astype(jnp.float32)).astype(bf16)
    return mixed[None]


def solution(mesh):
    in_specs = (
        P("section", "expert", None),
        P("section", None),
        P("section", None, "expert"),
        P("section", None, "expert"),
        P("section", "expert", None),
        P("section", "expert", None),
        P("section", "expert", None),
    )
    out_specs = P("section", "expert", None)
    return jax.shard_map(
        per_device, mesh=mesh, in_specs=in_specs, out_specs=out_specs, check_vma=False
    )
```

```python
import functools

import jax
import jax.numpy as jnp
from jax import lax
from jax.experimental import pallas as pl
from jax.experimental.pallas import tpu as pltpu
from jax.sharding import PartitionSpec as P

ROUTE_SCALE = 2.5
EPSILON = 1e-06
NY = 4
NZ = 8
SLICES = 4
LANES = 128
BF16 = jnp.bfloat16
F32 = jnp.float32
VMEM_BYTES = 48 * 1024 * 1024


def moved(x, dy, dz):
    sections = lax.axis_size("section")
    pairs = []
    for s in range(sections):
        sign = 1 if s % 2 == 0 else -1
        for y in range(NY):
            for z in range(NZ):
                to = ((y + sign * dy) % NY) * NZ + (z + sign * dz) % NZ
                pairs.append((s * NY * NZ + y * NZ + z, s * NY * NZ + to))
    return lax.ppermute(x, ("section", "expert"), pairs)


def next_section(x):
    size = lax.axis_size("section")
    return lax.ppermute(x, "section", [(i, (i + 1) % size) for i in range(size)])


def rms_normed(values, gain_row):
    widened = values.astype(F32)
    scaled = lax.rsqrt(jnp.mean(widened * widened, axis=-1, keepdims=True) + EPSILON)
    return (widened * scaled * gain_row).astype(BF16)


def route_weights(scores):
    gate_values = jax.nn.sigmoid(scores)
    return ROUTE_SCALE * gate_values / jnp.sum(gate_values, axis=-1, keepdims=True)


def dot(a, b):
    return jnp.dot(a, b, preferred_element_type=F32)


def after(x, *others):
    return lax.optimization_barrier((x, *others))[0]


def route_lanes(routes, logits, experts):
    hits = routes[:, :, None] == jnp.arange(experts, dtype=jnp.int32)
    weight = jnp.sum(hits.astype(F32) * route_weights(logits)[:, :, None], axis=1)
    named = jnp.sum(hits.astype(jnp.int32), axis=1)
    slot = jnp.where(named > 0, jnp.cumsum(named, axis=0) - 1, -1).astype(F32)
    high = lax.reduce_precision(weight, 8, 7)
    middle = lax.reduce_precision(weight - high, 8, 7)
    low = weight - high - middle
    parts = jnp.concatenate([high, middle, low, slot], axis=1).astype(BF16)
    return jnp.pad(parts, ((0, 0), (0, LANES - parts.shape[1])))


def lane_choice(columns, experts):
    lane = jnp.arange(LANES, dtype=jnp.int32)[None, :]
    expert = columns[:, None]
    weight = (lane == expert) | (lane == experts + expert) | (lane == 2 * experts + expert)
    slot = lane == 3 * experts + expert
    rows = jnp.concatenate([weight, slot], axis=0).astype(BF16)
    return jnp.pad(rows, ((0, LANES - rows.shape[0]), (0, 0)))


def hidden_kernel(blocks, part, tokens, seats, *refs):
    x_refs, choice_ref = refs[:blocks], refs[blocks]
    w_refs = refs[blocks + 1 : blocks + 1 + NY]
    out_refs = refs[blocks + 1 + NY : blocks + 1 + 2 * NY]
    picked_ref = refs[-1]
    rows = NY * tokens
    slots = NY * seats
    hid = w_refs[0].shape[1] // 2
    choice = choice_ref[...]
    number = lax.broadcasted_iota(jnp.int32, (slots, rows), 0)
    first = lax.broadcasted_iota(jnp.int32, (1, rows), 1) // tokens * seats
    for s in (2, 1, 3, 0):
        for b in range(blocks):
            info = lax.dot_general(
                choice,
                x_refs[b][:, part:],
                (((1,), (1,)), ((), ())),
                preferred_element_type=F32,
            )
            slot = info[NY + s : NY + s + 1, :].astype(jnp.int32)
            code = jnp.where(slot < 0, -1, slot + first)
            select = (number == code).astype(F32).astype(BF16)
            picked_ref[b * slots : (b + 1) * slots, :] = dot(select, x_refs[b][...]).astype(BF16)
        info = lax.dot_general(
            picked_ref[:, part:], choice, (((1,), (1,)), ((), ())), preferred_element_type=F32
        )
        sums = dot(picked_ref[:, :part], w_refs[s][...])
        dtype = out_refs[s].dtype
        out_refs[s][:, :hid] = sums[:, :hid].astype(dtype)
        out_refs[s][:, hid:] = (sums[:, hid:] * info[:, s : s + 1]).astype(dtype)


def hidden_partials(rows, choice, weights, tokens, seats):
    blocks = len(rows)
    part = weights[0].shape[0]
    hid2 = weights[0].shape[1]
    slots = NY * seats
    spec = pl.BlockSpec(memory_space=pltpu.VMEM)
    shape = (blocks * slots, hid2)
    kinds = (F32, F32, BF16, BF16)
    flops = 2 * NY * blocks * slots * part * (hid2 + NY * tokens)
    return pl.pallas_call(
        functools.partial(hidden_kernel, blocks, part, tokens, seats),
        out_shape=[jax.ShapeDtypeStruct(shape, kind) for kind in kinds],
        in_specs=[spec] * (blocks + 1 + NY),
        out_specs=[spec] * NY,
        scratch_shapes=[pltpu.VMEM((blocks * slots, part + LANES), BF16)],
        compiler_params=pltpu.CompilerParams(vmem_limit_bytes=VMEM_BYTES),
        cost_estimate=pl.CostEstimate(
            flops=flops, bytes_accessed=NY * part * hid2 * 2, transcendentals=0
        ),
    )(*rows, choice, *weights)


def down_kernel(part, tokens, seats, arriving, *refs):
    x_ref, choice_ref = refs[:2]
    act_refs = refs[2 : 2 + NY]
    w_refs = refs[2 + NY : 2 + 2 * NY]
    sent_refs = refs[2 + 2 * NY : 2 + 2 * NY + arriving]
    out_ref = refs[-2]
    wide_ref = refs[-1]
    rows = NY * tokens
    slots = NY * seats
    hid = act_refs[0].shape[1]
    info = lax.dot_general(
        x_ref[...], choice_ref[...], (((1,), (1,)), ((), ())), preferred_element_type=F32
    )
    number = lax.broadcasted_iota(jnp.int32, (rows, slots), 1)
    first = lax.broadcasted_iota(jnp.int32, (rows, 1), 0) // tokens * seats
    for s in range(NY):
        slot = info[:, NY + s : NY + s + 1].astype(jnp.int32)
        code = jnp.where(slot < 0, -1, slot + first)
        select = (number == code).astype(F32).astype(BF16)
        wide_ref[:, s * hid : (s + 1) * hid] = dot(select, act_refs[s][...]).astype(BF16)
    step = 256
    for c in range(0, part, step):
        total = dot(wide_ref[:, :hid], w_refs[0][:, c : c + step])
        for s in range(1, NY):
            total += dot(wide_ref[:, s * hid : (s + 1) * hid], w_refs[s][:, c : c + step])
        for sent in sent_refs:
            total += sent[:, c : c + step].astype(F32)
        out_ref[:, c : c + step] = total.astype(BF16)


def down_sums(lanes, choice, acts, weights, sent, tokens, seats):
    hid, part = weights[0].shape
    rows = NY * tokens
    spec = pl.BlockSpec(memory_space=pltpu.VMEM)
    return pl.pallas_call(
        functools.partial(down_kernel, part, tokens, seats, len(sent)),
        out_shape=jax.ShapeDtypeStruct((rows, part), BF16),
        in_specs=[spec] * (2 + 2 * NY + len(sent)),
        out_specs=spec,
        scratch_shapes=[pltpu.VMEM((rows, NY * hid), BF16)],
        compiler_params=pltpu.CompilerParams(vmem_limit_bytes=VMEM_BYTES),
        cost_estimate=pl.CostEstimate(
            flops=2 * rows * part * NY * hid,
            bytes_accessed=2 * part * (NY * hid + rows),
            transcendentals=0,
        ),
    )(lanes, choice, *acts, *weights, *sent)


def per_device(hidden, norm_gain, gate_weight, up_weight, down_weight, routes, logits):
    me = lax.axis_index("expert")
    odd = lax.axis_index("section") % 2
    y = jnp.where(odd == 1, (NY - me // NZ) % NY, me // NZ)
    tokens, width = hidden.shape[1], hidden.shape[2]
    top = routes.shape[2]
    hid = gate_weight.shape[2]
    part = width // NY
    experts = lax.axis_size("expert") // SLICES
    seats = 2 * tokens * top // experts
    gate, up, down = gate_weight[0], up_weight[0], down_weight[0]

    def place(d):
        return (y + d) % NY

    def gate_up_for(d):
        rows = (place(d) * part, 0)
        return jnp.concatenate(
            [lax.dynamic_slice(w, rows, (part, hid)) for w in (gate, up)], axis=1
        )

    def down_for(d):
        return lax.dynamic_slice(down, (0, place(d) * part), (hid, part))

    w_down = {0: down_for(0), 1: moved(down_for(3), -1, 0), 3: moved(down_for(1), 1, 0)}

    lanes = route_lanes(routes[0], logits[0], experts)
    there = (jnp.arange(NY, dtype=jnp.int32) * jnp.where(odd == 1, -1, 1) + me // NZ) % NY
    choice = lane_choice(there * (NZ // SLICES) + me % NZ // SLICES, experts)
    arrived = next_section(hidden[0])
    normed = rms_normed(arrived, norm_gain[0])

    def quarter(d):
        rows = lax.dynamic_slice(normed, (0, place(d) * part), (tokens, part))
        return jnp.concatenate([rows, lanes], axis=1)

    block = jnp.stack(
        [
            quarter(0),
            moved(quarter(3), -1, 0),
            moved(quarter(2), 2, 0),
            moved(quarter(1), 1, 0),
        ]
    )
    block = jnp.roll(block, y, axis=0).reshape(NY * tokens, part + LANES)
    x = {0: block}
    for k in (1, 2, 3):
        x[k] = moved(x[k - 1], 0, -1)
        x[-k] = moved(x[1 - k], 0, 1)
    x[4] = moved(x[3], 0, -1)

    w_gu = {0: gate_up_for(0)}
    w_gu[2] = moved(after(gate_up_for(2), block), 2, 0)
    w_gu[1] = moved(after(gate_up_for(3), block), -1, 0)
    w_gu[3] = moved(after(gate_up_for(1), block), 1, 0)
    w_down[2] = moved(after(down_for(2), x[2]), 2, 0)
    w_gu = [w_gu[s] for s in range(NY)]
    w_down = [w_down[s] for s in range(NY)]

    slots = NY * seats
    acts = {}
    before = None
    for keys in ((4,), (3, -3), (2, -2), (1, -1, 0)):
        rows = [x[k] for k in keys]
        if before is not None:
            rows[0] = after(rows[0], before)
        own, near, far, left = hidden_partials(rows, choice, w_gu, tokens, seats)
        before = far
        near = (near + moved(far, 1, 0).astype(F32)).astype(BF16)
        total = own + moved(near, 1, 0).astype(F32) + moved(left, -1, 0).astype(F32)
        act = (jax.nn.silu(total[:, :hid]) * total[:, hid:]).astype(BF16)
        all_acts = [act, moved(act, -1, 0), moved(act, 2, 0), moved(act, 1, 0)]
        for i, k in enumerate(keys):
            acts[k] = [a[i * slots : (i + 1) * slots] for a in all_acts]

    def sums(k, sent):
        return down_sums(x[k][:, part:], choice, acts[k], w_down, sent, tokens, seats)

    plus = moved(sums(4, []), 0, 1)
    minus = None
    for k in (3, 2, 1):
        plus = moved(sums(k, [plus]), 0, 1)
        minus = moved(sums(-k, [] if minus is None else [minus]), 0, -1)
    home = sums(0, [plus, minus]).reshape(NY, tokens, part)

    def rows_for(d):
        return lax.dynamic_index_in_dim(home, place(d), 0, keepdims=False)

    routed = jnp.stack(
        [
            rows_for(0),
            moved(rows_for(3), -1, 0),
            moved(rows_for(2), 2, 0),
            moved(rows_for(1), 1, 0),
        ]
    )
    routed = jnp.roll(routed, y, axis=0).transpose(1, 0, 2).reshape(tokens, width)
    mixed = (arrived.astype(F32) + routed.astype(F32)).astype(BF16)
    return mixed[None]


def solution(mesh):
    in_specs = (
        P("section", "expert", None),
        P("section", None),
        P("section", None, "expert"),
        P("section", None, "expert"),
        P("section", "expert", None),
        P("section", "expert", None),
        P("section", "expert", None),
    )
    out_specs = P("section", "expert", None)
    return jax.shard_map(
        per_device, mesh=mesh, in_specs=in_specs, out_specs=out_specs, check_vma=False
    )
```

```python
import functools

import jax
import jax.numpy as jnp
from jax import lax
from jax.experimental import pallas as pl
from jax.experimental.pallas import tpu as pltpu
from jax.sharding import PartitionSpec as P

ROUTE_SCALE = 2.5
EPSILON = 1e-06
NY = 4
NZ = 8
SLICES = 4
LANES = 128
BF16 = jnp.bfloat16
F32 = jnp.float32
VMEM_BYTES = 48 * 1024 * 1024


def moved(x, dy, dz):
    sections = lax.axis_size("section")
    pairs = []
    for s in range(sections):
        sign = 1 if s % 2 == 0 else -1
        for y in range(NY):
            for z in range(NZ):
                to = ((y + sign * dy) % NY) * NZ + (z + sign * dz) % NZ
                pairs.append((s * NY * NZ + y * NZ + z, s * NY * NZ + to))
    return lax.ppermute(x, ("section", "expert"), pairs)


def next_section(x):
    size = lax.axis_size("section")
    return lax.ppermute(x, "section", [(i, (i + 1) % size) for i in range(size)])


def rms_normed(values, gain_row):
    widened = values.astype(F32)
    scaled = lax.rsqrt(jnp.mean(widened * widened, axis=-1, keepdims=True) + EPSILON)
    return (widened * scaled * gain_row).astype(BF16)


def route_weights(scores):
    gate_values = jax.nn.sigmoid(scores)
    return ROUTE_SCALE * gate_values / jnp.sum(gate_values, axis=-1, keepdims=True)


def dot(a, b):
    return jnp.dot(a, b, preferred_element_type=F32)


def after(x, *others):
    return lax.optimization_barrier((x, *others))[0]


def route_lanes(routes, logits, experts):
    hits = routes[:, :, None] == jnp.arange(experts, dtype=jnp.int32)
    weight = jnp.sum(hits.astype(F32) * route_weights(logits)[:, :, None], axis=1)
    named = jnp.sum(hits.astype(jnp.int32), axis=1)
    slot = jnp.where(named > 0, jnp.cumsum(named, axis=0) - 1, -1).astype(F32)
    high = lax.reduce_precision(weight, 8, 7)
    middle = lax.reduce_precision(weight - high, 8, 7)
    low = weight - high - middle
    parts = jnp.concatenate([high, middle, low, slot], axis=1).astype(BF16)
    return jnp.pad(parts, ((0, 0), (0, LANES - parts.shape[1])))


def lane_choice(columns, experts):
    lane = jnp.arange(LANES, dtype=jnp.int32)[None, :]
    expert = columns[:, None]
    weight = (lane == expert) | (lane == experts + expert) | (lane == 2 * experts + expert)
    slot = lane == 3 * experts + expert
    rows = jnp.concatenate([weight, slot], axis=0).astype(BF16)
    return jnp.pad(rows, ((0, LANES - rows.shape[0]), (0, 0)))


def hidden_kernel(blocks, part, tokens, seats, *refs):
    x_refs, choice_ref = refs[:blocks], refs[blocks]
    gate_refs = refs[blocks + 1 : blocks + 1 + NY]
    up_refs = refs[blocks + 1 + NY : blocks + 1 + 2 * NY]
    out_refs = refs[blocks + 1 + 2 * NY : blocks + 1 + 3 * NY]
    picked_ref = refs[-1]
    rows = NY * tokens
    slots = NY * seats
    hid = gate_refs[0].shape[1]
    choice = choice_ref[...]
    number = lax.broadcasted_iota(jnp.int32, (slots, rows), 0)
    first = lax.broadcasted_iota(jnp.int32, (1, rows), 1) // tokens * seats
    for s in (2, 1, 3, 0):
        for b in range(blocks):
            info = lax.dot_general(
                choice,
                x_refs[b][:, part:],
                (((1,), (1,)), ((), ())),
                preferred_element_type=F32,
            )
            slot = info[NY + s : NY + s + 1, :].astype(jnp.int32)
            code = jnp.where(slot < 0, -1, slot + first)
            select = (number == code).astype(F32).astype(BF16)
            picked_ref[b * slots : (b + 1) * slots, :] = dot(select, x_refs[b][...]).astype(BF16)
        info = lax.dot_general(
            picked_ref[:, part:], choice, (((1,), (1,)), ((), ())), preferred_element_type=F32
        )
        dtype = out_refs[s].dtype
        gate = dot(picked_ref[:, :part], gate_refs[s][...])
        out_refs[s][:, :hid] = gate.astype(dtype)
        up = dot(picked_ref[:, :part], up_refs[s][...])
        out_refs[s][:, hid:] = (up * info[:, s : s + 1]).astype(dtype)


def hidden_partials(rows, choice, gates, ups, tokens, seats):
    blocks = len(rows)
    part = gates[0].shape[0]
    hid2 = 2 * gates[0].shape[1]
    slots = NY * seats
    spec = pl.BlockSpec(memory_space=pltpu.VMEM)
    shape = (blocks * slots, hid2)
    kinds = (F32, BF16, BF16, BF16)
    flops = 2 * NY * blocks * slots * part * (hid2 + NY * tokens)
    return pl.pallas_call(
        functools.partial(hidden_kernel, blocks, part, tokens, seats),
        out_shape=[jax.ShapeDtypeStruct(shape, kind) for kind in kinds],
        in_specs=[spec] * (blocks + 1 + 2 * NY),
        out_specs=[spec] * NY,
        scratch_shapes=[pltpu.VMEM((blocks * slots, part + LANES), BF16)],
        compiler_params=pltpu.CompilerParams(vmem_limit_bytes=VMEM_BYTES),
        cost_estimate=pl.CostEstimate(
            flops=flops, bytes_accessed=NY * part * hid2 * 2, transcendentals=0
        ),
    )(*rows, choice, *gates, *ups)


def down_kernel(part, tokens, seats, arriving, *refs):
    x_ref, choice_ref = refs[:2]
    act_refs = refs[2 : 2 + NY]
    w_refs = refs[2 + NY : 2 + 2 * NY]
    sent_refs = refs[2 + 2 * NY : 2 + 2 * NY + arriving]
    out_ref = refs[-2]
    wide_ref = refs[-1]
    rows = NY * tokens
    slots = NY * seats
    hid = act_refs[0].shape[1]
    info = lax.dot_general(
        x_ref[...], choice_ref[...], (((1,), (1,)), ((), ())), preferred_element_type=F32
    )
    number = lax.broadcasted_iota(jnp.int32, (rows, slots), 1)
    first = lax.broadcasted_iota(jnp.int32, (rows, 1), 0) // tokens * seats
    for s in range(NY):
        slot = info[:, NY + s : NY + s + 1].astype(jnp.int32)
        code = jnp.where(slot < 0, -1, slot + first)
        select = (number == code).astype(F32).astype(BF16)
        wide_ref[:, s * hid : (s + 1) * hid] = dot(select, act_refs[s][...]).astype(BF16)
    step = 256
    for c in range(0, part, step):
        total = dot(wide_ref[:, :hid], w_refs[0][:, c : c + step])
        for s in range(1, NY):
            total += dot(wide_ref[:, s * hid : (s + 1) * hid], w_refs[s][:, c : c + step])
        for sent in sent_refs:
            total += sent[:, c : c + step].astype(F32)
        out_ref[:, c : c + step] = total.astype(BF16)


def down_sums(block, choice, acts, weights, sent, tokens, seats):
    hid, part = weights[0].shape
    rows = NY * tokens
    spec = pl.BlockSpec(memory_space=pltpu.VMEM)
    lanes = pl.BlockSpec((rows, LANES), lambda i: (0, part // LANES))
    return pl.pallas_call(
        functools.partial(down_kernel, part, tokens, seats, len(sent)),
        out_shape=jax.ShapeDtypeStruct((rows, part), BF16),
        grid=(1,),
        in_specs=[lanes] + [spec] * (1 + 2 * NY + len(sent)),
        out_specs=spec,
        scratch_shapes=[pltpu.VMEM((rows, NY * hid), BF16)],
        compiler_params=pltpu.CompilerParams(vmem_limit_bytes=VMEM_BYTES),
        cost_estimate=pl.CostEstimate(
            flops=2 * rows * part * NY * hid,
            bytes_accessed=2 * part * (NY * hid + rows),
            transcendentals=0,
        ),
    )(block, choice, *acts, *weights, *sent)


def per_device(hidden, norm_gain, gate_weight, up_weight, down_weight, routes, logits):
    me = lax.axis_index("expert")
    odd = lax.axis_index("section") % 2
    y = jnp.where(odd == 1, (NY - me // NZ) % NY, me // NZ)
    tokens, width = hidden.shape[1], hidden.shape[2]
    top = routes.shape[2]
    hid = gate_weight.shape[2]
    part = width // NY
    experts = lax.axis_size("expert") // SLICES
    seats = 2 * tokens * top // experts
    gate, up, down = gate_weight[0], up_weight[0], down_weight[0]

    def place(d):
        return (y + d) % NY

    def in_for(weight, d):
        return lax.dynamic_slice(weight, (place(d) * part, 0), (part, hid))

    def down_for(d):
        return lax.dynamic_slice(down, (0, place(d) * part), (hid, part))

    w_down = {0: down_for(0), 1: moved(down_for(3), -1, 0), 3: moved(down_for(1), 1, 0)}

    lanes = route_lanes(routes[0], logits[0], experts)
    there = (jnp.arange(NY, dtype=jnp.int32) * jnp.where(odd == 1, -1, 1) + me // NZ) % NY
    choice = lane_choice(there * (NZ // SLICES) + me % NZ // SLICES, experts)
    arrived = next_section(hidden[0])
    normed = rms_normed(arrived, norm_gain[0])

    def quarter(d):
        rows = lax.dynamic_slice(normed, (0, place(d) * part), (tokens, part))
        return jnp.concatenate([rows, lanes], axis=1)

    block = jnp.stack(
        [
            quarter(0),
            moved(quarter(3), -1, 0),
            moved(quarter(2), 2, 0),
            moved(quarter(1), 1, 0),
        ]
    )
    block = jnp.roll(block, y, axis=0).reshape(NY * tokens, part + LANES)

    x = {0: block}
    gates, ups = {0: in_for(gate, 0)}, {0: in_for(up, 0)}
    pieces = ((gates, gate, (2,)), (gates, gate, (1, 3)), (ups, up, (2,)), (ups, up, (1, 3)))
    ahead = [block]
    for k, (kept, weight, distances) in enumerate(pieces, 1):
        slices = [in_for(weight, NY - d) for d in distances]
        slices, forth, back, _ = lax.optimization_barrier((slices, x[k - 1], x[1 - k], ahead))
        x[k] = moved(forth, 0, -1)
        if k < NZ // 2:
            x[-k] = moved(back, 0, 1)
        for d, w in zip(distances, slices):
            kept[d] = moved(w, -d, 0)
        ahead = [x[k], x.get(-k, x[k])] + [kept[d] for d in distances]
    w_down[2] = moved(lax.optimization_barrier((down_for(2), ahead))[0], 2, 0)
    gates, ups, w_down = ([w[s] for s in range(NY)] for w in (gates, ups, w_down))

    slots = NY * seats
    acts = {}

    def partials(keys, *earlier):
        rows = [after(x[k], *earlier) for k in keys]
        own, *rest = hidden_partials(rows, choice, gates, ups, tokens, seats)
        return own, [moved(r, s, 0) for s, r in enumerate(rest, 1)]

    def activate(keys, sums, *earlier):
        total = after(sums[0], *earlier)
        for r in sums[1]:
            total = total + r.astype(F32)
        act = (jax.nn.silu(total[:, :hid]) * total[:, hid:]).astype(BF16)
        everyone = [act] + [moved(act, -s, 0) for s in range(1, NY)]
        for i, k in enumerate(keys):
            acts[k] = [a[i * slots : (i + 1) * slots] for a in everyone]
        return act

    def down_of(k, sent, *earlier):
        block_acts = [after(acts[k][0], *earlier)] + acts[k][1:]
        return down_sums(x[k], choice, block_acts, w_down, sent, tokens, seats)

    g4, g3, g2, g1 = (4,), (3, -3), (2, -2), (1, -1, 0)
    h4 = partials(g4)
    h3 = partials(g3, h4[0])
    a4 = activate(g4, h4, h3[0])
    h2 = partials(g2, a4)
    s4 = down_of(4, [], h2[0])
    plus = moved(s4, 0, 1)
    a3 = activate(g3, h3, s4)
    h1 = partials(g1, a3)
    s3, r3 = down_of(3, [plus], h1[0]), down_of(-3, [], h1[0])
    plus, minus = moved(s3, 0, 1), moved(r3, 0, -1)
    a2 = activate(g2, h2, s3, r3)
    activate(g1, h1, a2)
    for k in (2, 1):
        plus, minus = moved(down_of(k, [plus]), 0, 1), moved(down_of(-k, [minus]), 0, -1)
    home = down_of(0, [plus, minus]).reshape(NY, tokens, part)

    def rows_for(d):
        return lax.dynamic_index_in_dim(home, place(d), 0, keepdims=False)

    routed = jnp.stack(
        [
            rows_for(0),
            moved(rows_for(3), -1, 0),
            moved(rows_for(2), 2, 0),
            moved(rows_for(1), 1, 0),
        ]
    )
    routed = jnp.roll(routed, y, axis=0).transpose(1, 0, 2).reshape(tokens, width)
    mixed = (arrived.astype(F32) + routed.astype(F32)).astype(BF16)
    return mixed[None]


def solution(mesh):
    in_specs = (
        P("section", "expert", None),
        P("section", None),
        P("section", None, "expert"),
        P("section", None, "expert"),
        P("section", "expert", None),
        P("section", "expert", None),
        P("section", "expert", None),
    )
    out_specs = P("section", "expert", None)
    return jax.shard_map(
        per_device, mesh=mesh, in_specs=in_specs, out_specs=out_specs, check_vma=False
    )
```

```python
import functools

import jax
import jax.numpy as jnp
from jax import lax
from jax.experimental import pallas as pl
from jax.experimental.pallas import tpu as pltpu
from jax.sharding import PartitionSpec as P

ROUTE_SCALE = 2.5
EPSILON = 1e-06
NY = 4
NZ = 8
SLICES = 4
LANES = 128
BF16 = jnp.bfloat16
F32 = jnp.float32
VMEM_BYTES = 48 * 1024 * 1024


def moved(x, dy, dz):
    sections = lax.axis_size("section")
    pairs = []
    for s in range(sections):
        sign = 1 if s % 2 == 0 else -1
        for y in range(NY):
            for z in range(NZ):
                to = ((y + sign * dy) % NY) * NZ + (z + sign * dz) % NZ
                pairs.append((s * NY * NZ + y * NZ + z, s * NY * NZ + to))
    return lax.ppermute(x, ("section", "expert"), pairs)


def next_section(x):
    size = lax.axis_size("section")
    return lax.ppermute(x, "section", [(i, (i + 1) % size) for i in range(size)])


def rms_normed(values, gain_row):
    widened = values.astype(F32)
    scaled = lax.rsqrt(jnp.mean(widened * widened, axis=-1, keepdims=True) + EPSILON)
    return (widened * scaled * gain_row).astype(BF16)


def route_weights(scores):
    gate_values = jax.nn.sigmoid(scores)
    return ROUTE_SCALE * gate_values / jnp.sum(gate_values, axis=-1, keepdims=True)


def dot(a, b):
    return jnp.dot(a, b, preferred_element_type=F32)


def after(x, *others):
    return lax.optimization_barrier((x, *others))[0]


def route_lanes(routes, logits, experts):
    hits = routes[:, :, None] == jnp.arange(experts, dtype=jnp.int32)
    weight = jnp.sum(hits.astype(F32) * route_weights(logits)[:, :, None], axis=1)
    named = jnp.sum(hits.astype(jnp.int32), axis=1)
    slot = jnp.where(named > 0, jnp.cumsum(named, axis=0) - 1, -1).astype(F32)
    high = lax.reduce_precision(weight, 8, 7)
    middle = lax.reduce_precision(weight - high, 8, 7)
    low = weight - high - middle
    parts = jnp.concatenate([high, middle, low, slot], axis=1).astype(BF16)
    return jnp.pad(parts, ((0, 0), (0, LANES - parts.shape[1])))


def lane_choice(columns, experts):
    lane = jnp.arange(LANES, dtype=jnp.int32)[None, :]
    expert = columns[:, None]
    weight = (lane == expert) | (lane == experts + expert) | (lane == 2 * experts + expert)
    slot = lane == 3 * experts + expert
    rows = jnp.concatenate([weight, slot], axis=0).astype(BF16)
    return jnp.pad(rows, ((0, LANES - rows.shape[0]), (0, 0)))


def hidden_kernel(blocks, part, tokens, seats, devices, *refs):
    x_refs, choice_ref = refs[:blocks], refs[blocks]
    count = len(devices)
    w_refs = refs[blocks + 1 : blocks + 1 + count]
    out_refs = refs[blocks + 1 + count : blocks + 1 + 2 * count]
    picked_ref = refs[-1]
    rows = NY * tokens
    slots = NY * seats
    hid = w_refs[0].shape[1] // 2
    choice = choice_ref[...]
    number = lax.broadcasted_iota(jnp.int32, (slots, rows), 0)
    first = lax.broadcasted_iota(jnp.int32, (1, rows), 1) // tokens * seats
    for s, w_ref, out_ref in zip(devices, w_refs, out_refs):
        for b in range(blocks):
            info = lax.dot_general(
                choice,
                x_refs[b][:, part:],
                (((1,), (1,)), ((), ())),
                preferred_element_type=F32,
            )
            slot = info[NY + s : NY + s + 1, :].astype(jnp.int32)
            code = jnp.where(slot < 0, -1, slot + first)
            select = (number == code).astype(F32).astype(BF16)
            picked_ref[b * slots : (b + 1) * slots, :] = dot(select, x_refs[b][...]).astype(BF16)
        info = lax.dot_general(
            picked_ref[:, part:], choice, (((1,), (1,)), ((), ())), preferred_element_type=F32
        )
        sums = dot(picked_ref[:, :part], w_ref[...])
        out_ref[:, :hid] = sums[:, :hid].astype(out_ref.dtype)
        out_ref[:, hid:] = (sums[:, hid:] * info[:, s : s + 1]).astype(out_ref.dtype)


def hidden_partials(rows, choice, weights, devices, tokens, seats):
    blocks = len(rows)
    part, hid2 = weights[devices[0]].shape
    slots = NY * seats
    spec = pl.BlockSpec(memory_space=pltpu.VMEM)
    shape = (blocks * slots, hid2)
    count = len(devices)
    return pl.pallas_call(
        functools.partial(hidden_kernel, blocks, part, tokens, seats, devices),
        out_shape=[jax.ShapeDtypeStruct(shape, F32 if s == 0 else BF16) for s in devices],
        in_specs=[spec] * (blocks + 1 + count),
        out_specs=[spec] * count,
        scratch_shapes=[pltpu.VMEM((blocks * slots, part + LANES), BF16)],
        compiler_params=pltpu.CompilerParams(vmem_limit_bytes=VMEM_BYTES),
        cost_estimate=pl.CostEstimate(
            flops=2 * count * blocks * slots * part * (hid2 + NY * tokens),
            bytes_accessed=count * part * hid2 * 2,
            transcendentals=0,
        ),
    )(*rows, choice, *[weights[s] for s in devices])


def down_kernel(part, tokens, seats, arriving, *refs):
    x_ref, choice_ref = refs[:2]
    act_refs = refs[2 : 2 + NY]
    w_refs = refs[2 + NY : 2 + 2 * NY]
    sent_refs = refs[2 + 2 * NY : 2 + 2 * NY + arriving]
    out_ref = refs[-2]
    wide_ref = refs[-1]
    rows = NY * tokens
    slots = NY * seats
    hid = act_refs[0].shape[1]
    info = lax.dot_general(
        x_ref[...], choice_ref[...], (((1,), (1,)), ((), ())), preferred_element_type=F32
    )
    number = lax.broadcasted_iota(jnp.int32, (rows, slots), 1)
    first = lax.broadcasted_iota(jnp.int32, (rows, 1), 0) // tokens * seats
    for s in range(NY):
        slot = info[:, NY + s : NY + s + 1].astype(jnp.int32)
        code = jnp.where(slot < 0, -1, slot + first)
        select = (number == code).astype(F32).astype(BF16)
        wide_ref[:, s * hid : (s + 1) * hid] = dot(select, act_refs[s][...]).astype(BF16)
    wide = out_ref.shape[1]
    for c in range(0, wide, 256):
        columns = slice(c, min(c + 256, wide))
        total = dot(wide_ref[:, :hid], w_refs[0][:, columns])
        for s in range(1, NY):
            total += dot(wide_ref[:, s * hid : (s + 1) * hid], w_refs[s][:, columns])
        for sent in sent_refs:
            total += sent[:, columns].astype(F32)
        out_ref[:, columns] = total.astype(BF16)


def down_sums(block, choice, acts, weights, half, sent, tokens, seats):
    hid, part = weights[0].shape
    rows = NY * tokens
    wide = part // 2
    spec = pl.BlockSpec(memory_space=pltpu.VMEM)
    lanes = pl.BlockSpec((rows, LANES), lambda i: (0, part // LANES))
    columns = pl.BlockSpec((hid, wide), lambda i: (0, half))
    return pl.pallas_call(
        functools.partial(down_kernel, part, tokens, seats, len(sent)),
        out_shape=jax.ShapeDtypeStruct((rows, wide), BF16),
        grid=(1,),
        in_specs=[lanes] + [spec] * (1 + NY) + [columns] * NY + [spec] * len(sent),
        out_specs=spec,
        scratch_shapes=[pltpu.VMEM((rows, NY * hid), BF16)],
        compiler_params=pltpu.CompilerParams(vmem_limit_bytes=VMEM_BYTES),
        cost_estimate=pl.CostEstimate(
            flops=2 * rows * wide * NY * hid,
            bytes_accessed=2 * wide * (NY * hid + rows),
            transcendentals=0,
        ),
    )(block, choice, *acts, *weights, *sent)


def per_device(hidden, norm_gain, gate_weight, up_weight, down_weight, routes, logits):
    me = lax.axis_index("expert")
    odd = lax.axis_index("section") % 2
    y = jnp.where(odd == 1, (NY - me // NZ) % NY, me // NZ)
    tokens, width = hidden.shape[1], hidden.shape[2]
    top = routes.shape[2]
    hid = gate_weight.shape[2]
    part = width // NY
    experts = lax.axis_size("expert") // SLICES
    seats = 2 * tokens * top // experts
    gate, up, down = gate_weight[0], up_weight[0], down_weight[0]

    def place(d):
        return (y + d) % NY

    def gate_up_for(d):
        rows = (place(d) * part, 0)
        return jnp.concatenate(
            [lax.dynamic_slice(w, rows, (part, hid)) for w in (gate, up)], axis=1
        )

    def down_for(d):
        return lax.dynamic_slice(down, (0, place(d) * part), (hid, part))

    w_down = {0: down_for(0), 1: moved(down_for(3), -1, 0), 3: moved(down_for(1), 1, 0)}

    lanes = route_lanes(routes[0], logits[0], experts)
    there = (jnp.arange(NY, dtype=jnp.int32) * jnp.where(odd == 1, -1, 1) + me // NZ) % NY
    choice = lane_choice(there * (NZ // SLICES) + me % NZ // SLICES, experts)
    arrived = next_section(hidden[0])
    ready, *_ = lax.optimization_barrier((arrived, w_down[1], w_down[3]))
    normed = rms_normed(ready, norm_gain[0])

    def quarter(d):
        rows = lax.dynamic_slice(normed, (0, place(d) * part), (tokens, part))
        return jnp.concatenate([rows, lanes], axis=1)

    block = jnp.stack(
        [
            quarter(0),
            moved(quarter(3), -1, 0),
            moved(quarter(2), 2, 0),
            moved(quarter(1), 1, 0),
        ]
    )
    block = jnp.roll(block, y, axis=0).reshape(NY * tokens, part + LANES)

    x = {0: block}
    w_in = {0: gate_up_for(0)}

    def step(k, forth, back):
        x[k] = moved(forth, 0, -1)
        if k < NZ // 2:
            x[-k] = moved(back, 0, 1)

    far, forth = lax.optimization_barrier((gate_up_for(2), block))
    w_in[2] = moved(far, 2, 0)
    step(1, forth, forth)
    step(2, x[1], x[-1])
    left, right, forth, back, far = lax.optimization_barrier(
        (gate_up_for(3), gate_up_for(1), x[2], x[-2], w_in[2])
    )
    w_in[1], w_in[3], w_in[2] = moved(left, -1, 0), moved(right, 1, 0), far
    step(3, forth, back)
    step(4, x[3], None)

    slots = NY * seats
    acts = {}

    def partials(keys, devices, *earlier):
        rows = [after(x[k], *earlier) for k in keys]
        return dict(zip(devices, hidden_partials(rows, choice, w_in, devices, tokens, seats)))

    def sent_out(sums):
        return [sums[0]] + [moved(sums[s], s, 0) for s in (1, 2, 3)]

    def activate(keys, sums, *earlier):
        total = after(sums[0], *earlier)
        for r in sums[1:]:
            total = total + r.astype(F32)
        act = (jax.nn.silu(total[:, :hid]) * total[:, hid:]).astype(BF16)
        everyone = [act] + [moved(act, -s, 0) for s in range(1, NY)]
        for i, k in enumerate(keys):
            acts[k] = [a[i * slots : (i + 1) * slots] for a in everyone]
        return act

    g4, g3, g2, g1 = (4,), (3, -3), (2, -2), (1, -1, 0)
    p1, p2, p3 = (partials(g, (0, 2)) for g in (g1, g2, g3))
    p4 = partials(g4, (2, 1, 3, 0), p1[0], p2[0], p3[0])
    down_2, _ = lax.optimization_barrier((down_for(2), p4[0]))
    h4 = sent_out(p4)
    w_down[2] = moved(down_2, 2, 0)
    w_down = [w_down[s] for s in range(NY)]

    def down_of(k, sent, *earlier):
        block_acts = [after(acts[k][0], *earlier)] + acts[k][1:]
        return [
            down_sums(x[k], choice, block_acts, w_down, c, [r[c] for r in sent], tokens, seats)
            for c in (0, 1)
        ]

    def on(sums, sign):
        return [moved(r, 0, sign) for r in sums]

    def rest_of(keys, early, *earlier):
        late = partials(keys, (1, 3), *earlier)
        return sent_out({0: early[0], 2: after(early[2], late[1]), **late}), late[1]

    h3, done = rest_of(g3, p3, p4[0])
    a4 = activate(g4, h4, done)
    h2, done = rest_of(g2, p2, a4)
    s4 = down_of(4, [], done)
    plus = on(s4, 1)
    a3 = activate(g3, h3, *s4)
    h1, done = rest_of(g1, p1, a3)
    s3, r3 = down_of(3, [plus], done), down_of(-3, [], done)
    plus, minus = on(s3, 1), on(r3, -1)
    a2 = activate(g2, h2, *s3, *r3)
    activate(g1, h1, a2)
    for k in (2, 1):
        s, r = down_of(k, [plus]), down_of(-k, [minus])
        plus, minus = on(s, 1), on(r, -1)
    halves = down_of(0, [plus, minus])

    def gathered(home):
        def rows_for(d):
            return lax.dynamic_index_in_dim(home, place(d), 0, keepdims=False)

        there = [rows_for(0)] + [moved(rows_for(NY - s), -s, 0) for s in range(1, NY)]
        return jnp.roll(jnp.stack(there), y, axis=0)

    routed = jnp.stack([gathered(h.reshape(NY, tokens, part // 2)) for h in halves])
    routed = routed.transpose(2, 1, 0, 3).reshape(tokens, width)
    mixed = (arrived.astype(F32) + routed.astype(F32)).astype(BF16)
    return mixed[None]


def solution(mesh):
    in_specs = (
        P("section", "expert", None),
        P("section", None),
        P("section", None, "expert"),
        P("section", None, "expert"),
        P("section", "expert", None),
        P("section", "expert", None),
        P("section", "expert", None),
    )
    out_specs = P("section", "expert", None)
    return jax.shard_map(
        per_device, mesh=mesh, in_specs=in_specs, out_specs=out_specs, check_vma=False
    )
```

```python
import functools

import jax
import jax.numpy as jnp
from jax import lax
from jax.experimental import pallas as pl
from jax.experimental.pallas import tpu as pltpu
from jax.sharding import PartitionSpec as P

ROUTE_SCALE = 2.5
EPSILON = 1e-06
NY = 4
NZ = 8
SLICES = 4
LANES = 128
BF16 = jnp.bfloat16
F32 = jnp.float32
VMEM_BYTES = 48 * 1024 * 1024


def moved(x, dy, dz):
    sections = lax.axis_size("section")
    pairs = []
    for s in range(sections):
        sign = 1 if s % 2 == 0 else -1
        for y in range(NY):
            for z in range(NZ):
                to = ((y + sign * dy) % NY) * NZ + (z + sign * dz) % NZ
                pairs.append((s * NY * NZ + y * NZ + z, s * NY * NZ + to))
    return lax.ppermute(x, ("section", "expert"), pairs)


def next_section(x, dy=0):
    sections = lax.axis_size("section")
    pairs = []
    for s in range(sections):
        to_section = (s + 1) % sections
        sign = 1 if to_section % 2 == 0 else -1
        for y in range(NY):
            for z in range(NZ):
                to = ((y + sign * dy) % NY) * NZ + z
                pairs.append((s * NY * NZ + y * NZ + z, to_section * NY * NZ + to))
    return lax.ppermute(x, ("section", "expert"), pairs)


def three_parts(x):
    high = lax.reduce_precision(x, 8, 7)
    middle = lax.reduce_precision(x - high, 8, 7)
    return [high, middle, x - high - middle]


def norm_factor(values):
    widened = values.astype(F32)
    return lax.rsqrt(jnp.mean(widened * widened, axis=-1, keepdims=True) + EPSILON)


def route_weights(scores):
    gate_values = jax.nn.sigmoid(scores)
    return ROUTE_SCALE * gate_values / jnp.sum(gate_values, axis=-1, keepdims=True)


def dot(a, b):
    return jnp.dot(a, b, preferred_element_type=F32)


def after(x, *others):
    return lax.optimization_barrier((x, *others))[0]


def route_lanes(routes, logits, experts):
    hits = routes[:, :, None] == jnp.arange(experts, dtype=jnp.int32)
    weight = jnp.sum(hits.astype(F32) * route_weights(logits)[:, :, None], axis=1)
    named = jnp.sum(hits.astype(jnp.int32), axis=1)
    slot = jnp.where(named > 0, jnp.cumsum(named, axis=0) - 1, -1).astype(F32)
    parts = jnp.concatenate(three_parts(weight) + [slot], axis=1).astype(BF16)
    return jnp.pad(parts, ((0, 0), (0, LANES - parts.shape[1])))


def lane_choice(columns, experts):
    lane = jnp.arange(LANES, dtype=jnp.int32)[None, :]
    expert = columns[:, None]
    weight = (lane == expert) | (lane == experts + expert) | (lane == 2 * experts + expert)
    slot = lane == 3 * experts + expert
    rows = jnp.concatenate([weight, slot], axis=0).astype(BF16)
    return jnp.pad(rows, ((0, LANES - rows.shape[0]), (0, 0)))


def block_kernel(part, y_ref, gain_ref, *refs):
    out_ref = refs[-1]
    tokens = refs[0].shape[0]
    for s in range(NY):
        row_ref, lane_ref = refs[s], refs[NY + s]
        home = pl.multiple_of(lax.rem(y_ref[0] + s, NY) * tokens, tokens)
        factor = row_ref[:, part:].astype(F32)
        factor = factor[:, :1] + factor[:, 1:2] + factor[:, 2:3]
        rows = row_ref[:, :part].astype(F32) * factor * gain_ref[...]
        out_ref[pl.ds(home, tokens), :part] = rows.astype(BF16)
        out_ref[pl.ds(home, tokens), part:] = lane_ref[...]


def normed_block(y, gain, rows, lanes):
    tokens, columns = rows[0].shape
    spec = pl.BlockSpec(memory_space=pltpu.VMEM)
    return pl.pallas_call(
        functools.partial(block_kernel, columns - LANES),
        out_shape=jax.ShapeDtypeStruct((NY * tokens, columns), BF16),
        in_specs=[pl.BlockSpec(memory_space=pltpu.SMEM)] + [spec] * (1 + 2 * NY),
        out_specs=spec,
        compiler_params=pltpu.CompilerParams(vmem_limit_bytes=VMEM_BYTES),
        cost_estimate=pl.CostEstimate(
            flops=2 * NY * tokens * columns,
            bytes_accessed=4 * NY * tokens * columns,
            transcendentals=0,
        ),
    )(y.reshape(1).astype(jnp.int32), gain, *rows, *lanes)


def hidden_kernel(blocks, part, tokens, seats, devices, *refs):
    x_refs, choice_ref = refs[:blocks], refs[blocks]
    count = len(devices)
    w_refs = refs[blocks + 1 : blocks + 1 + count]
    out_refs = refs[blocks + 1 + count : blocks + 1 + 2 * count]
    picked_ref = refs[-1]
    rows = NY * tokens
    slots = NY * seats
    hid = w_refs[0].shape[1] // 2
    choice = choice_ref[...]
    number = lax.broadcasted_iota(jnp.int32, (slots, rows), 0)
    first = lax.broadcasted_iota(jnp.int32, (1, rows), 1) // tokens * seats
    for s, w_ref, out_ref in zip(devices, w_refs, out_refs):
        for b in range(blocks):
            info = lax.dot_general(
                choice,
                x_refs[b][:, part:],
                (((1,), (1,)), ((), ())),
                preferred_element_type=F32,
            )
            slot = info[NY + s : NY + s + 1, :].astype(jnp.int32)
            code = jnp.where(slot < 0, -1, slot + first)
            select = (number == code).astype(F32).astype(BF16)
            picked_ref[b * slots : (b + 1) * slots, :] = dot(select, x_refs[b][...]).astype(BF16)
        info = lax.dot_general(
            picked_ref[:, part:], choice, (((1,), (1,)), ((), ())), preferred_element_type=F32
        )
        sums = dot(picked_ref[:, :part], w_ref[...])
        out_ref[:, :hid] = sums[:, :hid].astype(out_ref.dtype)
        out_ref[:, hid:] = (sums[:, hid:] * info[:, s : s + 1]).astype(out_ref.dtype)


def hidden_partials(rows, choice, weights, devices, tokens, seats):
    blocks = len(rows)
    part, hid2 = weights[devices[0]].shape
    slots = NY * seats
    spec = pl.BlockSpec(memory_space=pltpu.VMEM)
    shape = (blocks * slots, hid2)
    count = len(devices)
    return pl.pallas_call(
        functools.partial(hidden_kernel, blocks, part, tokens, seats, devices),
        out_shape=[jax.ShapeDtypeStruct(shape, F32 if s == 0 else BF16) for s in devices],
        in_specs=[spec] * (blocks + 1 + count),
        out_specs=[spec] * count,
        scratch_shapes=[pltpu.VMEM((blocks * slots, part + LANES), BF16)],
        compiler_params=pltpu.CompilerParams(vmem_limit_bytes=VMEM_BYTES),
        cost_estimate=pl.CostEstimate(
            flops=2 * count * blocks * slots * part * (hid2 + NY * tokens),
            bytes_accessed=count * part * hid2 * 2,
            transcendentals=0,
        ),
    )(*rows, choice, *[weights[s] for s in devices])


def down_kernel(part, tokens, seats, arriving, *refs):
    x_ref, choice_ref = refs[:2]
    act_refs = refs[2 : 2 + NY]
    w_refs = refs[2 + NY : 2 + 2 * NY]
    sent_refs = refs[2 + 2 * NY : 2 + 2 * NY + arriving]
    out_ref = refs[-2]
    wide_ref = refs[-1]
    rows = NY * tokens
    slots = NY * seats
    hid = act_refs[0].shape[1]
    info = lax.dot_general(
        x_ref[...], choice_ref[...], (((1,), (1,)), ((), ())), preferred_element_type=F32
    )
    number = lax.broadcasted_iota(jnp.int32, (rows, slots), 1)
    first = lax.broadcasted_iota(jnp.int32, (rows, 1), 0) // tokens * seats
    for s in range(NY):
        slot = info[:, NY + s : NY + s + 1].astype(jnp.int32)
        code = jnp.where(slot < 0, -1, slot + first)
        select = (number == code).astype(F32).astype(BF16)
        wide_ref[:, s * hid : (s + 1) * hid] = dot(select, act_refs[s][...]).astype(BF16)
    wide = out_ref.shape[1]
    for c in range(0, wide, 256):
        columns = slice(c, min(c + 256, wide))
        total = dot(wide_ref[:, :hid], w_refs[0][:, columns])
        for s in range(1, NY):
            total += dot(wide_ref[:, s * hid : (s + 1) * hid], w_refs[s][:, columns])
        for sent in sent_refs:
            total += sent[:, columns].astype(F32)
        out_ref[:, columns] = total.astype(BF16)


def down_sums(block, choice, acts, weights, half, sent, tokens, seats):
    hid, part = weights[0].shape
    rows = NY * tokens
    wide = part // 2
    spec = pl.BlockSpec(memory_space=pltpu.VMEM)
    lanes = pl.BlockSpec((rows, LANES), lambda i: (0, part // LANES))
    columns = pl.BlockSpec((hid, wide), lambda i: (0, half))
    return pl.pallas_call(
        functools.partial(down_kernel, part, tokens, seats, len(sent)),
        out_shape=jax.ShapeDtypeStruct((rows, wide), BF16),
        grid=(1,),
        in_specs=[lanes] + [spec] * (1 + NY) + [columns] * NY + [spec] * len(sent),
        out_specs=spec,
        scratch_shapes=[pltpu.VMEM((rows, NY * hid), BF16)],
        compiler_params=pltpu.CompilerParams(vmem_limit_bytes=VMEM_BYTES),
        cost_estimate=pl.CostEstimate(
            flops=2 * rows * wide * NY * hid,
            bytes_accessed=2 * wide * (NY * hid + rows),
            transcendentals=0,
        ),
    )(block, choice, *acts, *weights, *sent)


def per_device(hidden, norm_gain, gate_weight, up_weight, down_weight, routes, logits):
    me = lax.axis_index("expert")
    odd = lax.axis_index("section") % 2
    y = jnp.where(odd == 1, (NY - me // NZ) % NY, me // NZ)
    tokens, width = hidden.shape[1], hidden.shape[2]
    top = routes.shape[2]
    hid = gate_weight.shape[2]
    part = width // NY
    experts = lax.axis_size("expert") // SLICES
    seats = 2 * tokens * top // experts
    gate, up, down = gate_weight[0], up_weight[0], down_weight[0]

    def place(d):
        return (y + d) % NY

    def gate_up_for(d):
        rows = (place(d) * part, 0)
        return jnp.concatenate(
            [lax.dynamic_slice(w, rows, (part, hid)) for w in (gate, up)], axis=1
        )

    def down_for(d):
        return lax.dynamic_slice(down, (0, place(d) * part), (hid, part))

    w_down = {0: down_for(0), 1: moved(down_for(3), -1, 0), 3: moved(down_for(1), 1, 0)}

    lanes = route_lanes(routes[0], logits[0], experts)
    there = (jnp.arange(NY, dtype=jnp.int32) * jnp.where(odd == 1, -1, 1) + me // NZ) % NY
    choice = lane_choice(there * (NZ // SLICES) + me % NZ // SLICES, experts)
    parts = jnp.concatenate(three_parts(norm_factor(hidden[0])), axis=1).astype(BF16)
    parts = jnp.pad(parts, ((0, 0), (0, LANES - parts.shape[1])))
    there_y = (NY - y) % NY

    def quarter(d):
        first = (there_y + d) % NY * part
        rows = lax.dynamic_slice(hidden[0], (0, first), (tokens, part))
        return next_section(jnp.concatenate([rows, parts], axis=1), d)

    rows = [quarter((NY - s) % NY) for s in range(NY)]
    homes = [lanes] + [moved(lanes, NY - s, 0) for s in range(1, NY)]
    gain = lax.dynamic_slice(norm_gain, (0, y * part), (1, part))
    block = normed_block(y, gain, rows, homes)
    arrived = next_section(hidden[0])

    x = {0: block}
    w_in = {0: gate_up_for(0)}

    def step(k, forth, back):
        x[k] = moved(forth, 0, -1)
        if k < NZ // 2:
            x[-k] = moved(back, 0, 1)

    far, forth, w_down[1], w_down[3] = lax.optimization_barrier(
        (gate_up_for(2), block, w_down[1], w_down[3])
    )
    w_in[2] = moved(far, 2, 0)
    step(1, forth, forth)
    step(2, x[1], x[-1])
    left, right, forth, back, far, arrived = lax.optimization_barrier(
        (gate_up_for(3), gate_up_for(1), x[2], x[-2], w_in[2], arrived)
    )
    w_in[1], w_in[3], w_in[2] = moved(left, -1, 0), moved(right, 1, 0), far
    step(3, forth, back)
    forth, down_2 = lax.optimization_barrier((x[3], down_for(2)))
    step(4, forth, None)
    w_down[2] = moved(down_2, 2, 0)
    w_down = [w_down[s] for s in range(NY)]

    slots = NY * seats
    acts = {}

    def partials(keys, devices, *earlier):
        rows = [after(x[k], *earlier) for k in keys]
        return dict(zip(devices, hidden_partials(rows, choice, w_in, devices, tokens, seats)))

    def sent_out(sums):
        return [sums[0]] + [moved(sums[s], s, 0) for s in (1, 2, 3)]

    def activate(keys, sums, *earlier):
        total = after(sums[0], *earlier)
        for r in sums[1:]:
            total = total + r.astype(F32)
        act = (jax.nn.silu(total[:, :hid]) * total[:, hid:]).astype(BF16)
        everyone = [act] + [moved(act, -s, 0) for s in range(1, NY)]
        for i, k in enumerate(keys):
            acts[k] = [a[i * slots : (i + 1) * slots] for a in everyone]
        return act

    g4, g3, g2, g1 = (4,), (3, -3), (2, -2), (1, -1, 0)
    p1, p2, p3 = (partials(g, (0, 2)) for g in (g1, g2, g3))
    p4 = partials(g4, (2, 1, 3, 0), p1[0], p2[0], p3[0])
    h4 = sent_out(p4)

    def down_of(k, sent, *earlier):
        block_acts = [after(acts[k][0], *earlier)] + acts[k][1:]
        return [
            down_sums(x[k], choice, block_acts, w_down, c, [r[c] for r in sent], tokens, seats)
            for c in (0, 1)
        ]

    def on(sums, sign):
        return [moved(r, 0, sign) for r in sums]

    def rest_of(keys, early, *earlier):
        late = partials(keys, (1, 3), *earlier)
        return sent_out({0: early[0], 2: after(early[2], late[1]), **late}), late[1]

    h3, done = rest_of(g3, p3, p4[0])
    a4 = activate(g4, h4, done)
    h2, done = rest_of(g2, p2, a4)
    s4 = down_of(4, [], done)
    plus = on(s4, 1)
    a3 = activate(g3, h3, *s4)
    h1, done = rest_of(g1, p1, a3)
    s3, r3 = down_of(3, [plus], done), down_of(-3, [], done)
    plus, minus = on(s3, 1), on(r3, -1)
    a2 = activate(g2, h2, *s3, *r3)
    activate(g1, h1, a2)
    for k in (2, 1):
        s, r = down_of(k, [plus]), down_of(-k, [minus])
        plus, minus = on(s, 1), on(r, -1)
    halves = down_of(0, [plus, minus])

    def gathered(home):
        def rows_for(d):
            return lax.dynamic_index_in_dim(home, place(d), 0, keepdims=False)

        there = [rows_for(0)] + [moved(rows_for(NY - s), -s, 0) for s in range(1, NY)]
        return jnp.roll(jnp.stack(there), y, axis=0)

    routed = [gathered(h.reshape(NY, tokens, part // 2)) for h in halves]
    routed = jnp.concatenate(routed, axis=2).transpose(1, 0, 2).reshape(tokens, width)
    mixed = (arrived.astype(F32) + routed.astype(F32)).astype(BF16)
    return mixed[None]


def solution(mesh):
    in_specs = (
        P("section", "expert", None),
        P("section", None),
        P("section", None, "expert"),
        P("section", None, "expert"),
        P("section", "expert", None),
        P("section", "expert", None),
        P("section", "expert", None),
    )
    out_specs = P("section", "expert", None)
    return jax.shard_map(
        per_device, mesh=mesh, in_specs=in_specs, out_specs=out_specs, check_vma=False
    )
```

```python
import functools

import jax
import jax.numpy as jnp
from jax import lax
from jax.experimental import pallas as pl
from jax.experimental.pallas import tpu as pltpu
from jax.sharding import PartitionSpec as P

ROUTE_SCALE = 2.5
EPSILON = 1e-06
NY = 4
NZ = 8
SLICES = 4
LANES = 128
BF16 = jnp.bfloat16
F32 = jnp.float32
VMEM_BYTES = 48 * 1024 * 1024


def moved(x, dy, dz):
    sections = lax.axis_size("section")
    pairs = []
    for s in range(sections):
        sign = 1 if s % 2 == 0 else -1
        for y in range(NY):
            for z in range(NZ):
                to = ((y + sign * dy) % NY) * NZ + (z + sign * dz) % NZ
                pairs.append((s * NY * NZ + y * NZ + z, s * NY * NZ + to))
    return lax.ppermute(x, ("section", "expert"), pairs)


def next_section(x, dy=0):
    sections = lax.axis_size("section")
    pairs = []
    for s in range(sections):
        to_section = (s + 1) % sections
        sign = 1 if to_section % 2 == 0 else -1
        for y in range(NY):
            for z in range(NZ):
                to = ((y + sign * dy) % NY) * NZ + z
                pairs.append((s * NY * NZ + y * NZ + z, to_section * NY * NZ + to))
    return lax.ppermute(x, ("section", "expert"), pairs)


def three_parts(x):
    high = lax.reduce_precision(x, 8, 7)
    middle = lax.reduce_precision(x - high, 8, 7)
    return [high, middle, x - high - middle]


def route_weights(scores):
    gate_values = jax.nn.sigmoid(scores)
    return ROUTE_SCALE * gate_values / jnp.sum(gate_values, axis=-1, keepdims=True)


def dot(a, b):
    return jnp.dot(a, b, preferred_element_type=F32)


def after(x, *others):
    return lax.optimization_barrier((x, *others))[0]


def route_lanes(routes, logits, experts):
    hits = routes[:, :, None] == jnp.arange(experts, dtype=jnp.int32)
    weight = jnp.sum(hits.astype(F32) * route_weights(logits)[:, :, None], axis=1)
    named = jnp.sum(hits.astype(jnp.int32), axis=1)
    slot = jnp.where(named > 0, jnp.cumsum(named, axis=0) - 1, -1).astype(F32)
    parts = jnp.concatenate(three_parts(weight) + [slot], axis=1).astype(BF16)
    return jnp.pad(parts, ((0, 0), (0, LANES - parts.shape[1])))


def lane_choice(columns, experts):
    lane = jnp.arange(LANES, dtype=jnp.int32)[None, :]
    expert = columns[:, None]
    weight = (lane == expert) | (lane == experts + expert) | (lane == 2 * experts + expert)
    slot = lane == 3 * experts + expert
    rows = jnp.concatenate([weight, slot], axis=0).astype(BF16)
    return jnp.pad(rows, ((0, LANES - rows.shape[0]), (0, 0)))


def quarter_kernel(place_ref, x_ref, *out_refs):
    tokens, width = x_ref.shape
    part = width // NY
    widened = x_ref[...].astype(F32)
    mean = jnp.sum(widened * widened, axis=-1, keepdims=True) * (1.0 / width)
    factor = lax.rsqrt(mean + EPSILON)
    high = factor.astype(BF16).astype(F32)
    middle = (factor - high).astype(BF16).astype(F32)
    low = factor - high - middle
    lane = lax.broadcasted_iota(jnp.int32, (tokens, LANES), 1)
    lanes = jnp.where(lane == 0, high, jnp.where(lane == 1, middle, jnp.where(lane == 2, low, 0.0)))
    for s, out_ref in enumerate(out_refs):
        first = pl.multiple_of(place_ref[s] * part, LANES)
        out_ref[:, :part] = x_ref[:, pl.ds(first, part)]
        out_ref[:, part:] = lanes.astype(BF16)


def quarters_of(rows, places):
    tokens, width = rows.shape
    spec = pl.BlockSpec(memory_space=pltpu.VMEM)
    shape = jax.ShapeDtypeStruct((tokens, width // NY + LANES), BF16)
    return pl.pallas_call(
        quarter_kernel,
        out_shape=[shape] * NY,
        in_specs=[pl.BlockSpec(memory_space=pltpu.SMEM), spec],
        out_specs=[spec] * NY,
        compiler_params=pltpu.CompilerParams(vmem_limit_bytes=VMEM_BYTES),
        cost_estimate=pl.CostEstimate(
            flops=4 * tokens * width, bytes_accessed=4 * tokens * width, transcendentals=0
        ),
    )(places, rows)


def block_kernel(part, y_ref, gain_ref, *refs):
    out_ref = refs[-1]
    tokens = refs[0].shape[0]
    for s in range(NY):
        row_ref, lane_ref = refs[s], refs[NY + s]
        home = pl.multiple_of(lax.rem(y_ref[0] + s, NY) * tokens, tokens)
        factor = row_ref[:, part:].astype(F32)
        factor = factor[:, :1] + factor[:, 1:2] + factor[:, 2:3]
        rows = row_ref[:, :part].astype(F32) * factor * gain_ref[...]
        out_ref[pl.ds(home, tokens), :part] = rows.astype(BF16)
        out_ref[pl.ds(home, tokens), part:] = lane_ref[...]


def normed_block(y, gain, rows, lanes):
    tokens, columns = rows[0].shape
    spec = pl.BlockSpec(memory_space=pltpu.VMEM)
    return pl.pallas_call(
        functools.partial(block_kernel, columns - LANES),
        out_shape=jax.ShapeDtypeStruct((NY * tokens, columns), BF16),
        in_specs=[pl.BlockSpec(memory_space=pltpu.SMEM)] + [spec] * (1 + 2 * NY),
        out_specs=spec,
        compiler_params=pltpu.CompilerParams(vmem_limit_bytes=VMEM_BYTES),
        cost_estimate=pl.CostEstimate(
            flops=2 * NY * tokens * columns,
            bytes_accessed=4 * NY * tokens * columns,
            transcendentals=0,
        ),
    )(y.reshape(1).astype(jnp.int32), gain, *rows, *lanes)


def hidden_kernel(blocks, part, tokens, seats, devices, *refs):
    x_refs, choice_ref = refs[:blocks], refs[blocks]
    count = len(devices)
    w_refs = refs[blocks + 1 : blocks + 1 + count]
    out_refs = refs[blocks + 1 + count : blocks + 1 + 2 * count]
    picked_ref = refs[-1]
    rows = NY * tokens
    slots = NY * seats
    hid = w_refs[0].shape[1] // 2
    choice = choice_ref[...]
    number = lax.broadcasted_iota(jnp.int32, (slots, rows), 0)
    first = lax.broadcasted_iota(jnp.int32, (1, rows), 1) // tokens * seats
    for s, w_ref, out_ref in zip(devices, w_refs, out_refs):
        for b in range(blocks):
            info = lax.dot_general(
                choice,
                x_refs[b][:, part:],
                (((1,), (1,)), ((), ())),
                preferred_element_type=F32,
            )
            slot = info[NY + s : NY + s + 1, :].astype(jnp.int32)
            code = jnp.where(slot < 0, -1, slot + first)
            select = (number == code).astype(F32).astype(BF16)
            picked_ref[b * slots : (b + 1) * slots, :] = dot(select, x_refs[b][...]).astype(BF16)
        info = lax.dot_general(
            picked_ref[:, part:], choice, (((1,), (1,)), ((), ())), preferred_element_type=F32
        )
        sums = dot(picked_ref[:, :part], w_ref[...])
        out_ref[:, :hid] = sums[:, :hid].astype(out_ref.dtype)
        out_ref[:, hid:] = (sums[:, hid:] * info[:, s : s + 1]).astype(out_ref.dtype)


def hidden_partials(rows, choice, weights, devices, tokens, seats):
    blocks = len(rows)
    part, hid2 = weights[devices[0]].shape
    slots = NY * seats
    spec = pl.BlockSpec(memory_space=pltpu.VMEM)
    shape = (blocks * slots, hid2)
    count = len(devices)
    return pl.pallas_call(
        functools.partial(hidden_kernel, blocks, part, tokens, seats, devices),
        out_shape=[jax.ShapeDtypeStruct(shape, F32 if s == 0 else BF16) for s in devices],
        in_specs=[spec] * (blocks + 1 + count),
        out_specs=[spec] * count,
        scratch_shapes=[pltpu.VMEM((blocks * slots, part + LANES), BF16)],
        compiler_params=pltpu.CompilerParams(vmem_limit_bytes=VMEM_BYTES),
        cost_estimate=pl.CostEstimate(
            flops=2 * count * blocks * slots * part * (hid2 + NY * tokens),
            bytes_accessed=count * part * hid2 * 2,
            transcendentals=0,
        ),
    )(*rows, choice, *[weights[s] for s in devices])


def down_kernel(part, tokens, seats, arriving, *refs):
    x_ref, choice_ref = refs[:2]
    act_refs = refs[2 : 2 + NY]
    w_refs = refs[2 + NY : 2 + 2 * NY]
    sent_refs = refs[2 + 2 * NY : 2 + 2 * NY + arriving]
    out_ref = refs[-2]
    wide_ref = refs[-1]
    rows = NY * tokens
    slots = NY * seats
    hid = act_refs[0].shape[1]
    info = lax.dot_general(
        x_ref[...], choice_ref[...], (((1,), (1,)), ((), ())), preferred_element_type=F32
    )
    number = lax.broadcasted_iota(jnp.int32, (rows, slots), 1)
    first = lax.broadcasted_iota(jnp.int32, (rows, 1), 0) // tokens * seats
    for s in range(NY):
        slot = info[:, NY + s : NY + s + 1].astype(jnp.int32)
        code = jnp.where(slot < 0, -1, slot + first)
        select = (number == code).astype(F32).astype(BF16)
        wide_ref[:, s * hid : (s + 1) * hid] = dot(select, act_refs[s][...]).astype(BF16)
    wide = out_ref.shape[1]
    for c in range(0, wide, 256):
        columns = slice(c, min(c + 256, wide))
        total = dot(wide_ref[:, :hid], w_refs[0][:, columns])
        for s in range(1, NY):
            total += dot(wide_ref[:, s * hid : (s + 1) * hid], w_refs[s][:, columns])
        for sent in sent_refs:
            total += sent[:, columns].astype(F32)
        out_ref[:, columns] = total.astype(BF16)


def columns_of(rows, wide, at):
    return pl.BlockSpec((rows, wide), lambda i: (0, at))


def down_sums(block, choice, acts, weights, half, sent, tokens, seats):
    hid, part = weights[0].shape
    rows = NY * tokens
    wide, at = (part, 0) if half is None else (part // 2, half)
    spec = pl.BlockSpec(memory_space=pltpu.VMEM)
    lanes = pl.BlockSpec((rows, LANES), lambda i: (0, part // LANES))
    columns = columns_of(hid, wide, at)
    there = [columns_of(rows, wide, at if r.shape[1] == part else 0) for r in sent]
    return pl.pallas_call(
        functools.partial(down_kernel, part, tokens, seats, len(sent)),
        out_shape=jax.ShapeDtypeStruct((rows, wide), BF16),
        grid=(1,),
        in_specs=[lanes] + [spec] * (1 + NY) + [columns] * NY + there,
        out_specs=spec,
        scratch_shapes=[pltpu.VMEM((rows, NY * hid), BF16)],
        compiler_params=pltpu.CompilerParams(vmem_limit_bytes=VMEM_BYTES),
        cost_estimate=pl.CostEstimate(
            flops=2 * rows * wide * NY * hid,
            bytes_accessed=2 * wide * (NY * hid + rows),
            transcendentals=0,
        ),
    )(block, choice, *acts, *weights, *sent)


def per_device(hidden, norm_gain, gate_weight, up_weight, down_weight, routes, logits):
    me = lax.axis_index("expert")
    odd = lax.axis_index("section") % 2
    y = jnp.where(odd == 1, (NY - me // NZ) % NY, me // NZ)
    tokens, width = hidden.shape[1], hidden.shape[2]
    top = routes.shape[2]
    hid = gate_weight.shape[2]
    part = width // NY
    experts = lax.axis_size("expert") // SLICES
    seats = 2 * tokens * top // experts
    gate, up, down = gate_weight[0], up_weight[0], down_weight[0]

    def place(d):
        return (y + d) % NY

    def gate_up_for(d):
        rows = (place(d) * part, 0)
        return jnp.concatenate(
            [lax.dynamic_slice(w, rows, (part, hid)) for w in (gate, up)], axis=1
        )

    def down_for(d, *earlier):
        at = after(place(d), *earlier) if earlier else place(d)
        return lax.dynamic_slice(down, (0, at * part), (hid, part))

    there_y = (NY - y) % NY
    places = (there_y + NY - jnp.arange(NY, dtype=jnp.int32)) % NY
    rows = quarters_of(hidden[0], places.astype(jnp.int32))
    near, far = down_for(1, rows[0]), down_for(3, rows[0])
    rows = [next_section(r, (NY - s) % NY) for s, r in enumerate(rows)]
    w_down = {0: down_for(0), 1: moved(far, -1, 0), 3: moved(near, 1, 0)}
    lanes = route_lanes(routes[0], logits[0], experts)
    there = (jnp.arange(NY, dtype=jnp.int32) * jnp.where(odd == 1, -1, 1) + me // NZ) % NY
    choice = lane_choice(there * (NZ // SLICES) + me % NZ // SLICES, experts)
    homes = [lanes] + [moved(lanes, NY - s, 0) for s in range(1, NY)]
    gain = lax.dynamic_slice(norm_gain, (0, y * part), (1, part))
    block = normed_block(y, gain, rows, homes)
    arrived = next_section(hidden[0])

    x = {0: block}
    w_in = {0: gate_up_for(0)}

    def step(k, forth, back):
        x[k] = moved(forth, 0, -1)
        if k < NZ // 2:
            x[-k] = moved(back, 0, 1)

    far, forth, w_down[1], w_down[3] = lax.optimization_barrier(
        (gate_up_for(2), block, w_down[1], w_down[3])
    )
    w_in[2] = moved(far, 2, 0)
    step(1, forth, forth)
    step(2, x[1], x[-1])
    left, right, forth, back, far, arrived = lax.optimization_barrier(
        (gate_up_for(3), gate_up_for(1), x[2], x[-2], w_in[2], arrived)
    )
    w_in[1], w_in[3], w_in[2] = moved(left, -1, 0), moved(right, 1, 0), far
    step(3, forth, back)
    forth, down_2 = lax.optimization_barrier((x[3], down_for(2)))
    step(4, forth, None)
    w_down[2] = moved(down_2, 2, 0)
    w_down = [w_down[s] for s in range(NY)]

    slots = NY * seats
    acts = {}

    def partials(keys, devices, *earlier):
        rows = [after(x[k], *earlier) for k in keys]
        return dict(zip(devices, hidden_partials(rows, choice, w_in, devices, tokens, seats)))

    def sent_out(sums, *earlier):
        return [sums[0]] + [moved(after(sums[s], *earlier), s, 0) for s in (1, 2, 3)]

    def activate(keys, sums, *earlier):
        total = after(sums[0], *earlier)
        for r in sums[1:]:
            total = total + r.astype(F32)
        act = (jax.nn.silu(total[:, :hid]) * total[:, hid:]).astype(BF16)
        everyone = [act] + [moved(act, -s, 0) for s in range(1, NY)]
        for i, k in enumerate(keys):
            acts[k] = [a[i * slots : (i + 1) * slots] for a in everyone]
        return act

    def down_of(k, half, sent, *earlier):
        block_acts = [after(acts[k][0], *earlier)] + acts[k][1:]
        return down_sums(x[k], choice, block_acts, w_down, half, sent, tokens, seats)

    g4, g3, g2, g1 = (4,), (3, -3), (2, -2), (1, -1, 0)
    p1, p2, p3 = (partials(g, (0, 2)) for g in (g1, g2, g3))
    p4 = partials(g4, (2, 1, 3, 0), p1[0], p2[0], p3[0])
    p3.update(partials(g3, (1, 3), p4[0]))
    p2.update(partials(g2, (1, 3), p3[1]))
    h4 = sent_out(p4, p2[1])
    h3 = sent_out(p3, p2[1])
    p1.update(partials(g1, (1, 3), p2[1]))
    a4 = activate(g4, h4, p1[1])
    a3 = activate(g3, h3, a4)
    h2 = sent_out(p2, a3)
    s4 = down_of(4, None, [], a3)
    plus = moved(s4, 0, 1)
    h1 = sent_out(p1, s4)
    a2 = activate(g2, h2, s4)
    s3, r3 = down_of(3, None, [plus], a2), down_of(-3, None, [], a2)
    plus, minus = moved(s3, 0, 1), moved(r3, 0, -1)
    activate(g1, h1, s3, r3)
    plus = moved(down_of(2, None, [plus]), 0, 1)
    minus = moved(down_of(-2, None, [minus]), 0, -1)
    plus = [moved(down_of(1, c, [plus]), 0, 1) for c in (0, 1)]
    minus = [moved(down_of(-1, c, [minus]), 0, -1) for c in (0, 1)]
    halves = [down_of(0, c, [plus[c], minus[c]]) for c in (0, 1)]

    def gathered(home):
        def rows_for(d):
            return lax.dynamic_index_in_dim(home, place(d), 0, keepdims=False)

        there = [rows_for(0)] + [moved(rows_for(NY - s), -s, 0) for s in range(1, NY)]
        return jnp.roll(jnp.stack(there), y, axis=0)

    routed = [gathered(h.reshape(NY, tokens, part // 2)) for h in halves]
    routed = jnp.concatenate(routed, axis=2).transpose(1, 0, 2).reshape(tokens, width)
    mixed = (arrived.astype(F32) + routed.astype(F32)).astype(BF16)
    return mixed[None]


def solution(mesh):
    in_specs = (
        P("section", "expert", None),
        P("section", None),
        P("section", None, "expert"),
        P("section", None, "expert"),
        P("section", "expert", None),
        P("section", "expert", None),
        P("section", "expert", None),
    )
    out_specs = P("section", "expert", None)
    return jax.shard_map(
        per_device, mesh=mesh, in_specs=in_specs, out_specs=out_specs, check_vma=False
    )
```

```python
import functools

import jax
import jax.numpy as jnp
from jax import lax
from jax.experimental import pallas as pl
from jax.experimental.pallas import tpu as pltpu
from jax.sharding import PartitionSpec as P

ROUTE_SCALE = 2.5
EPSILON = 1e-06
NY = 4
NZ = 8
SLICES = 4
LANES = 128
BF16 = jnp.bfloat16
F32 = jnp.float32
VMEM_BYTES = 48 * 1024 * 1024
LITTLE = pl.CostEstimate(flops=1024, bytes_accessed=1024, transcendentals=0)


def moved(x, dy, dz):
    sections = lax.axis_size("section")
    pairs = []
    for s in range(sections):
        sign = 1 if s % 2 == 0 else -1
        for y in range(NY):
            for z in range(NZ):
                to = ((y + sign * dy) % NY) * NZ + (z + sign * dz) % NZ
                pairs.append((s * NY * NZ + y * NZ + z, s * NY * NZ + to))
    return lax.ppermute(x, ("section", "expert"), pairs)


def next_section(x, dy=0):
    sections = lax.axis_size("section")
    pairs = []
    for s in range(sections):
        to_section = (s + 1) % sections
        sign = 1 if to_section % 2 == 0 else -1
        for y in range(NY):
            for z in range(NZ):
                to = ((y + sign * dy) % NY) * NZ + z
                pairs.append((s * NY * NZ + y * NZ + z, to_section * NY * NZ + to))
    return lax.ppermute(x, ("section", "expert"), pairs)


def three_parts(x):
    high = lax.reduce_precision(x, 8, 7)
    middle = lax.reduce_precision(x - high, 8, 7)
    return [high, middle, x - high - middle]


def route_weights(scores):
    gate_values = jax.nn.sigmoid(scores)
    return ROUTE_SCALE * gate_values / jnp.sum(gate_values, axis=-1, keepdims=True)


def dot(a, b):
    return jnp.dot(a, b, preferred_element_type=F32)


def after(x, *others):
    return lax.optimization_barrier((x, *others))[0]


def route_lanes(routes, logits, experts):
    hits = routes[:, :, None] == jnp.arange(experts, dtype=jnp.int32)
    weight = jnp.sum(hits.astype(F32) * route_weights(logits)[:, :, None], axis=1)
    named = jnp.sum(hits.astype(jnp.int32), axis=1)
    slot = jnp.where(named > 0, jnp.cumsum(named, axis=0) - 1, -1).astype(F32)
    parts = jnp.concatenate(three_parts(weight) + [slot], axis=1).astype(BF16)
    return jnp.pad(parts, ((0, 0), (0, LANES - parts.shape[1])))


def lane_choice(columns, experts):
    lane = jnp.arange(LANES, dtype=jnp.int32)[None, :]
    expert = columns[:, None]
    weight = (lane == expert) | (lane == experts + expert) | (lane == 2 * experts + expert)
    slot = lane == 3 * experts + expert
    rows = jnp.concatenate([weight, slot], axis=0).astype(BF16)
    return jnp.pad(rows, ((0, LANES - rows.shape[0]), (0, 0)))


def quarter_kernel(place_ref, x_ref, *out_refs):
    tokens, width = x_ref.shape
    part = width // NY
    widened = x_ref[...].astype(F32)
    mean = jnp.sum(widened * widened, axis=-1, keepdims=True) * (1.0 / width)
    factor = lax.rsqrt(mean + EPSILON)
    high = factor.astype(BF16).astype(F32)
    middle = (factor - high).astype(BF16).astype(F32)
    low = factor - high - middle
    lane = lax.broadcasted_iota(jnp.int32, (tokens, LANES), 1)
    lanes = jnp.where(lane == 0, high, jnp.where(lane == 1, middle, jnp.where(lane == 2, low, 0.0)))
    for s, out_ref in enumerate(out_refs):
        first = pl.multiple_of(place_ref[s] * part, LANES)
        out_ref[:, :part] = x_ref[:, pl.ds(first, part)]
        out_ref[:, part:] = lanes.astype(BF16)


def quarters_of(rows, places):
    tokens, width = rows.shape
    spec = pl.BlockSpec(memory_space=pltpu.VMEM)
    shape = jax.ShapeDtypeStruct((tokens, width // NY + LANES), BF16)
    return pl.pallas_call(
        quarter_kernel,
        out_shape=[shape] * NY,
        in_specs=[pl.BlockSpec(memory_space=pltpu.SMEM), spec],
        out_specs=[spec] * NY,
        compiler_params=pltpu.CompilerParams(vmem_limit_bytes=VMEM_BYTES),
        cost_estimate=LITTLE,
    )(places, rows)


def block_kernel(part, y_ref, gain_ref, *refs):
    out_ref = refs[-1]
    tokens = refs[0].shape[0]
    for s in range(NY):
        row_ref, lane_ref = refs[s], refs[NY + s]
        home = pl.multiple_of(lax.rem(y_ref[0] + s, NY) * tokens, tokens)
        factor = row_ref[:, part:].astype(F32)
        factor = factor[:, :1] + factor[:, 1:2] + factor[:, 2:3]
        rows = row_ref[:, :part].astype(F32) * factor * gain_ref[...]
        out_ref[pl.ds(home, tokens), :part] = rows.astype(BF16)
        out_ref[pl.ds(home, tokens), part:] = lane_ref[...]


def normed_block(y, gain, rows, lanes):
    tokens, columns = rows[0].shape
    spec = pl.BlockSpec(memory_space=pltpu.VMEM)
    return pl.pallas_call(
        functools.partial(block_kernel, columns - LANES),
        out_shape=jax.ShapeDtypeStruct((NY * tokens, columns), BF16),
        in_specs=[pl.BlockSpec(memory_space=pltpu.SMEM)] + [spec] * (1 + 2 * NY),
        out_specs=spec,
        compiler_params=pltpu.CompilerParams(vmem_limit_bytes=VMEM_BYTES),
        cost_estimate=LITTLE,
    )(y.reshape(1).astype(jnp.int32), gain, *rows, *lanes)


def hidden_kernel(blocks, part, tokens, seats, devices, *refs):
    x_refs, choice_ref = refs[:blocks], refs[blocks]
    count = len(devices)
    w_refs = refs[blocks + 1 : blocks + 1 + count]
    out_refs = refs[blocks + 1 + count : blocks + 1 + 2 * count]
    picked_ref = refs[-1]
    rows = NY * tokens
    slots = NY * seats
    hid = w_refs[0].shape[1] // 2
    choice = choice_ref[...]
    number = lax.broadcasted_iota(jnp.int32, (slots, rows), 0)
    first = lax.broadcasted_iota(jnp.int32, (1, rows), 1) // tokens * seats
    for s, w_ref, out_ref in zip(devices, w_refs, out_refs):
        for b in range(blocks):
            info = lax.dot_general(
                choice,
                x_refs[b][:, part:],
                (((1,), (1,)), ((), ())),
                preferred_element_type=F32,
            )
            slot = info[NY + s : NY + s + 1, :].astype(jnp.int32)
            code = jnp.where(slot < 0, -1, slot + first)
            select = (number == code).astype(F32).astype(BF16)
            picked_ref[b * slots : (b + 1) * slots, :] = dot(select, x_refs[b][...]).astype(BF16)
        info = lax.dot_general(
            picked_ref[:, part:], choice, (((1,), (1,)), ((), ())), preferred_element_type=F32
        )
        sums = dot(picked_ref[:, :part], w_ref[...])
        out_ref[:, :hid] = sums[:, :hid].astype(out_ref.dtype)
        out_ref[:, hid:] = (sums[:, hid:] * info[:, s : s + 1]).astype(out_ref.dtype)


def hidden_partials(rows, choice, weights, devices, tokens, seats):
    blocks = len(rows)
    part, hid2 = weights[devices[0]].shape
    slots = NY * seats
    spec = pl.BlockSpec(memory_space=pltpu.VMEM)
    shape = (blocks * slots, hid2)
    count = len(devices)
    return pl.pallas_call(
        functools.partial(hidden_kernel, blocks, part, tokens, seats, devices),
        out_shape=[jax.ShapeDtypeStruct(shape, F32 if s == 0 else BF16) for s in devices],
        in_specs=[spec] * (blocks + 1 + count),
        out_specs=[spec] * count,
        scratch_shapes=[pltpu.VMEM((blocks * slots, part + LANES), BF16)],
        compiler_params=pltpu.CompilerParams(vmem_limit_bytes=VMEM_BYTES),
        cost_estimate=LITTLE,
    )(*rows, choice, *[weights[s] for s in devices])


def down_kernel(part, tokens, seats, x_ref, choice_ref, *refs):
    act_refs, w_refs = refs[:NY], refs[NY : 2 * NY]
    out_ref, wide_ref = refs[-2:]
    rows = NY * tokens
    slots = NY * seats
    hid = act_refs[0].shape[1]
    info = lax.dot_general(
        x_ref[...], choice_ref[...], (((1,), (1,)), ((), ())), preferred_element_type=F32
    )
    number = lax.broadcasted_iota(jnp.int32, (rows, slots), 1)
    first = lax.broadcasted_iota(jnp.int32, (rows, 1), 0) // tokens * seats
    for s in range(NY):
        slot = info[:, NY + s : NY + s + 1].astype(jnp.int32)
        code = jnp.where(slot < 0, -1, slot + first)
        select = (number == code).astype(F32).astype(BF16)
        wide_ref[:, s * hid : (s + 1) * hid] = dot(select, act_refs[s][...]).astype(BF16)
    for c in range(0, part, 256):
        columns = slice(c, min(c + 256, part))
        total = dot(wide_ref[:, :hid], w_refs[0][:, columns])
        for s in range(1, NY):
            total += dot(wide_ref[:, s * hid : (s + 1) * hid], w_refs[s][:, columns])
        out_ref[:, columns] = total.astype(out_ref.dtype)


def down_sums(block, choice, acts, at, weights, kind, tokens, seats):
    hid, part = weights[0].shape
    rows = NY * tokens
    slots = NY * seats
    spec = pl.BlockSpec(memory_space=pltpu.VMEM)
    lanes = pl.BlockSpec((rows, LANES), lambda i: (0, part // LANES))
    group = pl.BlockSpec((slots, hid), lambda i: (at, 0))
    return pl.pallas_call(
        functools.partial(down_kernel, part, tokens, seats),
        out_shape=jax.ShapeDtypeStruct((rows, part), kind),
        grid=(1,),
        in_specs=[lanes, spec] + [group] * NY + [spec] * NY,
        out_specs=spec,
        scratch_shapes=[pltpu.VMEM((rows, NY * hid), BF16)],
        compiler_params=pltpu.CompilerParams(vmem_limit_bytes=VMEM_BYTES),
        cost_estimate=LITTLE,
    )(block, choice, *acts, *weights)


def per_device(hidden, norm_gain, gate_weight, up_weight, down_weight, routes, logits):
    me = lax.axis_index("expert")
    odd = lax.axis_index("section") % 2
    y = jnp.where(odd == 1, (NY - me // NZ) % NY, me // NZ)
    tokens, width = hidden.shape[1], hidden.shape[2]
    top = routes.shape[2]
    hid = gate_weight.shape[2]
    part = width // NY
    experts = lax.axis_size("expert") // SLICES
    seats = 2 * tokens * top // experts
    gate, up, down = gate_weight[0], up_weight[0], down_weight[0]

    def place(d):
        return (y + d) % NY

    there_y = (NY - y) % NY
    places = (there_y + NY - jnp.arange(NY, dtype=jnp.int32)) % NY
    outgoing = quarters_of(hidden[0], places.astype(jnp.int32))
    rows = [next_section(r, (NY - s) % NY) for s, r in enumerate(outgoing)]
    lanes = route_lanes(*lax.optimization_barrier((routes[0], logits[0], outgoing[0]))[:2], experts)
    there = (jnp.arange(NY, dtype=jnp.int32) * jnp.where(odd == 1, -1, 1) + me // NZ) % NY
    choice = lane_choice(there * (NZ // SLICES) + me % NZ // SLICES, experts)
    homes = [lanes] + [moved(lanes, NY - s, 0) for s in range(1, NY)]
    gain = lax.dynamic_slice(norm_gain, (0, y * part), (1, part))
    block = normed_block(y, gain, rows, homes)
    arrived = next_section(hidden[0])

    def gate_up_for(d, *earlier):
        start = (after(place(d), *earlier) * part, 0)
        return jnp.concatenate(
            [lax.dynamic_slice(w, start, (part, hid)) for w in (gate, up)], axis=1
        )

    def down_for(d, *earlier):
        return lax.dynamic_slice(down, (0, after(place(d), *earlier) * part), (hid, part))

    x = {0: block}

    def step(k, forth, back):
        x[k] = moved(forth, 0, -1)
        if k < NZ // 2:
            x[-k] = moved(back, 0, 1)

    barrier = lax.optimization_barrier
    far, near, left, forth = barrier(
        (
            gate_up_for(2, *homes[1:]),
            down_for(1, *homes[1:]),
            down_for(3, *homes[1:]),
            block,
        )
    )
    w_down = {1: moved(left, -1, 0), 3: moved(near, 1, 0)}
    w_in = {2: moved(far, 2, 0)}
    step(1, forth, forth)
    forth, back, w_down[1], w_down[3] = barrier((x[1], x[-1], w_down[1], w_down[3]))
    step(2, forth, back)
    w_in[0], w_down[0] = gate_up_for(0, x[1]), down_for(0, x[1])
    left, near, forth, back, w_in[2], arrived = barrier(
        (gate_up_for(3, x[1]), gate_up_for(1, x[1]), x[2], x[-2], w_in[2], arrived)
    )
    w_in[1], w_in[3] = moved(left, -1, 0), moved(near, 1, 0)
    step(3, forth, back)
    forth, far = barrier((x[3], down_for(2, x[1])))
    step(4, forth, None)
    w_down[2] = moved(far, 2, 0)
    w_down = [w_down[s] for s in range(NY)]

    acts = {}

    def partials(keys, devices, *earlier):
        rows = [after(x[k], *earlier) for k in keys]
        return dict(zip(devices, hidden_partials(rows, choice, w_in, devices, tokens, seats)))

    def sent_out(sums, *earlier):
        return [sums[0]] + [moved(after(sums[s], *earlier), s, 0) for s in (1, 2, 3)]

    def activate(keys, sums, *earlier):
        total = after(sums[0], *earlier)
        for r in sums[1:]:
            total = total + r.astype(F32)
        act = (jax.nn.silu(total[:, :hid]) * total[:, hid:]).astype(BF16)
        everyone = [act] + [moved(act, -s, 0) for s in range(1, NY)]
        for i, k in enumerate(keys):
            acts[k] = (everyone, i)
        return act

    def down_of(k, kind, *earlier):
        group, at = acts[k]
        group = [after(group[0], *earlier)] + group[1:]
        return down_sums(x[k], choice, group, at, w_down, kind, tokens, seats)

    def plus_sent(own, *sent):
        for r in sent:
            own = own + r.astype(F32)
        return own.astype(BF16)

    g3, g2, g1 = (4, 3, -3), (2, -2), (1, -1, 0)
    p1, p2 = (partials(g, (0, 2)) for g in (g1, g2))
    p3 = partials(g3, (2, 1, 3, 0), p1[0], p2[0])
    p2.update(partials(g2, (1, 3), p3[0]))
    h3 = sent_out(p3, p2[1], w_down[2])
    p1.update(partials(g1, (1, 3), p2[1]))
    a3 = activate(g3, h3, p1[1])
    h2 = sent_out(p2, a3)
    s4 = down_of(4, BF16)
    r3 = down_of(-3, BF16, s4)
    plus, minus = moved(s4, 0, 1), moved(r3, 0, -1)
    h1 = sent_out(p1, r3)
    s3 = down_of(3, F32, r3)
    a2 = activate(g2, h2, s3)
    plus = moved(plus_sent(after(s3, a2), plus), 0, 1)
    a1 = activate(g1, h1, a2)
    s2, r2 = down_of(2, F32), down_of(-2, F32)
    plus = moved(plus_sent(s2, plus), 0, 1)
    minus = moved(plus_sent(r2, minus), 0, -1)
    s1, r1 = down_of(1, F32, s2, r2), down_of(-1, F32, s2, r2)
    s0 = down_of(0, F32, s1, r1)
    wide = part // 2
    halves = []
    for c in (slice(0, wide), slice(wide, part)):
        ahead = moved(plus_sent(s1[:, c], plus[:, c]), 0, 1)
        behind = moved(plus_sent(r1[:, c], minus[:, c]), 0, -1)
        halves.append(plus_sent(s0[:, c], ahead, behind))

    def gathered(home):
        def rows_for(d):
            return lax.dynamic_index_in_dim(home, place(d), 0, keepdims=False)

        there = [rows_for(0)] + [moved(rows_for(NY - s), -s, 0) for s in range(1, NY)]
        return jnp.roll(jnp.stack(there), y, axis=0)

    routed = [gathered(h.reshape(NY, tokens, part // 2)) for h in halves]
    routed = jnp.concatenate(routed, axis=2).transpose(1, 0, 2).reshape(tokens, width)
    mixed = (arrived.astype(F32) + routed.astype(F32)).astype(BF16)
    return mixed[None]


def solution(mesh):
    in_specs = (
        P("section", "expert", None),
        P("section", None),
        P("section", None, "expert"),
        P("section", None, "expert"),
        P("section", "expert", None),
        P("section", "expert", None),
        P("section", "expert", None),
    )
    out_specs = P("section", "expert", None)
    return jax.shard_map(
        per_device, mesh=mesh, in_specs=in_specs, out_specs=out_specs, check_vma=False
    )
```

```python
import functools

import jax
import jax.numpy as jnp
from jax import lax
from jax.experimental import pallas as pl
from jax.experimental.pallas import tpu as pltpu
from jax.sharding import PartitionSpec as P

ROUTE_SCALE = 2.5
EPSILON = 1e-06
NY = 4
NZ = 8
SLICES = 4
LANES = 128
BF16 = jnp.bfloat16
F32 = jnp.float32
VMEM_BYTES = 48 * 1024 * 1024
LITTLE = pl.CostEstimate(flops=1024, bytes_accessed=1024, transcendentals=0)


def moved(x, dy, dz):
    sections = lax.axis_size("section")
    pairs = []
    for s in range(sections):
        sign = 1 if s % 2 == 0 else -1
        for y in range(NY):
            for z in range(NZ):
                to = ((y + sign * dy) % NY) * NZ + (z + sign * dz) % NZ
                pairs.append((s * NY * NZ + y * NZ + z, s * NY * NZ + to))
    return lax.ppermute(x, ("section", "expert"), pairs)


def next_section(x, dy=0):
    sections = lax.axis_size("section")
    pairs = []
    for s in range(sections):
        to_section = (s + 1) % sections
        sign = 1 if to_section % 2 == 0 else -1
        for y in range(NY):
            for z in range(NZ):
                to = ((y + sign * dy) % NY) * NZ + z
                pairs.append((s * NY * NZ + y * NZ + z, to_section * NY * NZ + to))
    return lax.ppermute(x, ("section", "expert"), pairs)


def three_parts(x):
    high = lax.reduce_precision(x, 8, 7)
    middle = lax.reduce_precision(x - high, 8, 7)
    return [high, middle, x - high - middle]


def route_weights(scores):
    gate_values = jax.nn.sigmoid(scores)
    return ROUTE_SCALE * gate_values / jnp.sum(gate_values, axis=-1, keepdims=True)


def dot(a, b):
    return jnp.dot(a, b, preferred_element_type=F32)


def after(x, *others):
    return lax.optimization_barrier((x, *others))[0]


def route_lanes(routes, logits, experts):
    hits = routes[:, :, None] == jnp.arange(experts, dtype=jnp.int32)
    weight = jnp.sum(hits.astype(F32) * route_weights(logits)[:, :, None], axis=1)
    named = jnp.sum(hits.astype(jnp.int32), axis=1)
    slot = jnp.where(named > 0, jnp.cumsum(named, axis=0) - 1, -1).astype(F32)
    parts = jnp.concatenate(three_parts(weight) + [slot], axis=1).astype(BF16)
    return jnp.pad(parts, ((0, 0), (0, LANES - parts.shape[1])))


def lane_choice(columns, experts):
    lane = jnp.arange(LANES, dtype=jnp.int32)[None, :]
    expert = columns[:, None]
    weight = (lane == expert) | (lane == experts + expert) | (lane == 2 * experts + expert)
    slot = lane == 3 * experts + expert
    rows = jnp.concatenate([weight, slot], axis=0).astype(BF16)
    return jnp.pad(rows, ((0, LANES - rows.shape[0]), (0, 0)))


def quarter_kernel(place_ref, x_ref, *out_refs):
    tokens, width = x_ref.shape
    part = width // NY
    widened = x_ref[...].astype(F32)
    mean = jnp.sum(widened * widened, axis=-1, keepdims=True) * (1.0 / width)
    factor = lax.rsqrt(mean + EPSILON)
    high = factor.astype(BF16).astype(F32)
    middle = (factor - high).astype(BF16).astype(F32)
    low = factor - high - middle
    lane = lax.broadcasted_iota(jnp.int32, (tokens, LANES), 1)
    lanes = jnp.where(lane == 0, high, jnp.where(lane == 1, middle, jnp.where(lane == 2, low, 0.0)))
    for s, out_ref in enumerate(out_refs):
        first = pl.multiple_of(place_ref[s] * part, LANES)
        out_ref[:, :part] = x_ref[:, pl.ds(first, part)]
        out_ref[:, part:] = lanes.astype(BF16)


def quarters_of(rows, places):
    tokens, width = rows.shape
    spec = pl.BlockSpec(memory_space=pltpu.VMEM)
    shape = jax.ShapeDtypeStruct((tokens, width // NY + LANES), BF16)
    return pl.pallas_call(
        quarter_kernel,
        out_shape=[shape] * NY,
        in_specs=[pl.BlockSpec(memory_space=pltpu.SMEM), spec],
        out_specs=[spec] * NY,
        compiler_params=pltpu.CompilerParams(vmem_limit_bytes=VMEM_BYTES),
        cost_estimate=LITTLE,
    )(places, rows)


def block_kernel(part, y_ref, gain_ref, *refs):
    out_ref = refs[-1]
    tokens = refs[0].shape[0]
    for s in range(NY):
        row_ref, lane_ref = refs[s], refs[NY + s]
        home = pl.multiple_of(lax.rem(y_ref[0] + s, NY) * tokens, tokens)
        factor = row_ref[:, part:].astype(F32)
        factor = factor[:, :1] + factor[:, 1:2] + factor[:, 2:3]
        rows = row_ref[:, :part].astype(F32) * factor * gain_ref[...]
        out_ref[pl.ds(home, tokens), :part] = rows.astype(BF16)
        out_ref[pl.ds(home, tokens), part:] = lane_ref[...]


def normed_block(y, gain, rows, lanes):
    tokens, columns = rows[0].shape
    spec = pl.BlockSpec(memory_space=pltpu.VMEM)
    return pl.pallas_call(
        functools.partial(block_kernel, columns - LANES),
        out_shape=jax.ShapeDtypeStruct((NY * tokens, columns), BF16),
        in_specs=[pl.BlockSpec(memory_space=pltpu.SMEM)] + [spec] * (1 + 2 * NY),
        out_specs=spec,
        compiler_params=pltpu.CompilerParams(vmem_limit_bytes=VMEM_BYTES),
        cost_estimate=LITTLE,
    )(y.reshape(1).astype(jnp.int32), gain, *rows, *lanes)


def hidden_kernel(blocks, part, tokens, seats, devices, *refs):
    x_refs, choice_ref = refs[:blocks], refs[blocks]
    count = len(devices)
    w_refs = refs[blocks + 1 : blocks + 1 + count]
    out_refs = refs[blocks + 1 + count : blocks + 1 + 2 * count]
    picked_ref = refs[-1]
    rows = NY * tokens
    slots = NY * seats
    hid = w_refs[0].shape[1] // 2
    choice = choice_ref[...]
    number = lax.broadcasted_iota(jnp.int32, (slots, rows), 0)
    first = lax.broadcasted_iota(jnp.int32, (1, rows), 1) // tokens * seats
    for s, w_ref, out_ref in zip(devices, w_refs, out_refs):
        for b in range(blocks):
            info = lax.dot_general(
                choice,
                x_refs[b][:, part:],
                (((1,), (1,)), ((), ())),
                preferred_element_type=F32,
            )
            slot = info[NY + s : NY + s + 1, :].astype(jnp.int32)
            code = jnp.where(slot < 0, -1, slot + first)
            select = (number == code).astype(F32).astype(BF16)
            picked_ref[b * slots : (b + 1) * slots, :] = dot(select, x_refs[b][...]).astype(BF16)
        info = lax.dot_general(
            picked_ref[:, part:], choice, (((1,), (1,)), ((), ())), preferred_element_type=F32
        )
        sums = dot(picked_ref[:, :part], w_ref[...])
        out_ref[:, :hid] = sums[:, :hid].astype(out_ref.dtype)
        out_ref[:, hid:] = (sums[:, hid:] * info[:, s : s + 1]).astype(out_ref.dtype)


def hidden_partials(rows, choice, weights, devices, tokens, seats):
    blocks = len(rows)
    part, hid2 = weights[devices[0]].shape
    slots = NY * seats
    spec = pl.BlockSpec(memory_space=pltpu.VMEM)
    shape = (blocks * slots, hid2)
    count = len(devices)
    return pl.pallas_call(
        functools.partial(hidden_kernel, blocks, part, tokens, seats, devices),
        out_shape=[jax.ShapeDtypeStruct(shape, F32 if s == 0 else BF16) for s in devices],
        in_specs=[spec] * (blocks + 1 + count),
        out_specs=[spec] * count,
        scratch_shapes=[pltpu.VMEM((blocks * slots, part + LANES), BF16)],
        compiler_params=pltpu.CompilerParams(vmem_limit_bytes=VMEM_BYTES),
        cost_estimate=LITTLE,
    )(*rows, choice, *[weights[s] for s in devices])


def down_kernel(part, tokens, seats, arriving, *refs):
    x_ref, choice_ref = refs[:2]
    act_refs = refs[2 : 2 + NY]
    w_refs = refs[2 + NY : 2 + 2 * NY]
    sent_refs = refs[2 + 2 * NY : 2 + 2 * NY + arriving]
    out_ref = refs[-2]
    wide_ref = refs[-1]
    rows = NY * tokens
    slots = NY * seats
    hid = act_refs[0].shape[1]
    info = lax.dot_general(
        x_ref[...], choice_ref[...], (((1,), (1,)), ((), ())), preferred_element_type=F32
    )
    number = lax.broadcasted_iota(jnp.int32, (rows, slots), 1)
    first = lax.broadcasted_iota(jnp.int32, (rows, 1), 0) // tokens * seats
    for s in range(NY):
        slot = info[:, NY + s : NY + s + 1].astype(jnp.int32)
        code = jnp.where(slot < 0, -1, slot + first)
        select = (number == code).astype(F32).astype(BF16)
        wide_ref[:, s * hid : (s + 1) * hid] = dot(select, act_refs[s][...]).astype(BF16)
    wide = out_ref.shape[1]
    for c in range(0, wide, 256):
        columns = slice(c, min(c + 256, wide))
        total = dot(wide_ref[:, :hid], w_refs[0][:, columns])
        for s in range(1, NY):
            total += dot(wide_ref[:, s * hid : (s + 1) * hid], w_refs[s][:, columns])
        for sent in sent_refs:
            total += sent[:, columns].astype(F32)
        out_ref[:, columns] = total.astype(BF16)


def columns_of(rows, wide, at):
    return pl.BlockSpec((rows, wide), lambda i: (0, at))


def down_sums(block, choice, acts, weights, half, sent, tokens, seats):
    hid, part = weights[0].shape
    rows = NY * tokens
    wide, at = (part, 0) if half is None else (part // 2, half)
    spec = pl.BlockSpec(memory_space=pltpu.VMEM)
    lanes = pl.BlockSpec((rows, LANES), lambda i: (0, part // LANES))
    columns = columns_of(hid, wide, at)
    there = [columns_of(rows, wide, at if r.shape[1] == part else 0) for r in sent]
    return pl.pallas_call(
        functools.partial(down_kernel, part, tokens, seats, len(sent)),
        out_shape=jax.ShapeDtypeStruct((rows, wide), BF16),
        grid=(1,),
        in_specs=[lanes] + [spec] * (1 + NY) + [columns] * NY + there,
        out_specs=spec,
        scratch_shapes=[pltpu.VMEM((rows, NY * hid), BF16)],
        compiler_params=pltpu.CompilerParams(vmem_limit_bytes=VMEM_BYTES),
        cost_estimate=LITTLE,
    )(block, choice, *acts, *weights, *sent)


def per_device(hidden, norm_gain, gate_weight, up_weight, down_weight, routes, logits):
    me = lax.axis_index("expert")
    odd = lax.axis_index("section") % 2
    y = jnp.where(odd == 1, (NY - me // NZ) % NY, me // NZ)
    tokens, width = hidden.shape[1], hidden.shape[2]
    top = routes.shape[2]
    hid = gate_weight.shape[2]
    part = width // NY
    experts = lax.axis_size("expert") // SLICES
    seats = 2 * tokens * top // experts
    gate, up, down = gate_weight[0], up_weight[0], down_weight[0]

    def place(d):
        return (y + d) % NY

    there_y = (NY - y) % NY
    places = (there_y + NY - jnp.arange(NY, dtype=jnp.int32)) % NY
    outgoing = quarters_of(hidden[0], places.astype(jnp.int32))
    rows = [next_section(r, (NY - s) % NY) for s, r in enumerate(outgoing)]
    lanes = route_lanes(*lax.optimization_barrier((routes[0], logits[0], outgoing[0]))[:2], experts)
    there = (jnp.arange(NY, dtype=jnp.int32) * jnp.where(odd == 1, -1, 1) + me // NZ) % NY
    choice = lane_choice(there * (NZ // SLICES) + me % NZ // SLICES, experts)
    homes = [lanes] + [moved(lanes, NY - s, 0) for s in range(1, NY)]
    gain = lax.dynamic_slice(norm_gain, (0, y * part), (1, part))
    block = normed_block(y, gain, rows, homes)
    arrived = next_section(hidden[0])

    def gate_up_for(d, *earlier):
        start = (after(place(d), *earlier) * part, 0)
        return jnp.concatenate(
            [lax.dynamic_slice(w, start, (part, hid)) for w in (gate, up)], axis=1
        )

    def down_for(d, *earlier):
        return lax.dynamic_slice(down, (0, after(place(d), *earlier) * part), (hid, part))

    x = {0: block}

    def step(k, forth, back):
        x[k] = moved(forth, 0, -1)
        if k < NZ // 2:
            x[-k] = moved(back, 0, 1)

    barrier = lax.optimization_barrier
    far, forth = barrier((gate_up_for(2, *homes[1:]), block))
    w_in = {2: moved(far, 2, 0)}
    step(1, forth, forth)
    step(2, x[1], x[-1])
    w_in[0], w_down = gate_up_for(0, x[1]), [down_for(0, x[1])]
    left, near, forth, back, w_in[2], arrived = barrier(
        (gate_up_for(3, x[1]), gate_up_for(1, x[1]), x[2], x[-2], w_in[2], arrived)
    )
    w_in[1], w_in[3] = moved(left, -1, 0), moved(near, 1, 0)
    step(3, forth, back)

    slots = NY * seats
    acts = {}

    def partials(keys, devices, *earlier):
        rows = [after(x[k], *earlier) for k in keys]
        return dict(zip(devices, hidden_partials(rows, choice, w_in, devices, tokens, seats)))

    def sent_out(sums, *earlier):
        return [sums[0]] + [moved(after(sums[s], *earlier), s, 0) for s in (1, 2, 3)]

    def activate(keys, sums, *earlier):
        total = after(sums[0], *earlier)
        for r in sums[1:]:
            total = total + r.astype(F32)
        act = (jax.nn.silu(total[:, :hid]) * total[:, hid:]).astype(BF16)
        everyone = [act] + [moved(act, -s, 0) for s in range(1, NY)]
        for i, k in enumerate(keys):
            acts[k] = (everyone, i)
        return act

    def down_of(k, half, sent, *earlier):
        group, at = acts[k]
        group = [after(group[0], *earlier)] + group[1:]
        block_acts = [a[at * slots : (at + 1) * slots] for a in group]
        return down_sums(x[k], choice, block_acts, w_down, half, sent, tokens, seats)

    g4, g3, g2, g1 = (4,), (3, -3), (2, -2), (1, -1, 0)
    p1, p2 = (partials(g, (0, 2)) for g in (g1, g2))
    downs = [down_for(NY - s, x[2]) for s in (1, 2, 3)]
    forth, downs, w_in[1], w_in[3], *_ = barrier(
        (x[3], downs, w_in[1], w_in[3], p1[0], p2[0])
    )
    step(4, forth, None)
    w_down += [moved(w, -s, 0) for s, w in enumerate(downs, 1)]
    p3 = partials(g3, (2, 1, 3, 0))
    p2.update(partials(g2, (1, 3), p3[0]))
    p1.update(partials(g1, (1, 3), p2[1]))
    p4 = partials(g4, (2, 1, 3, 0), p1[1])
    h4 = sent_out(p4, *w_down)
    h3 = sent_out(p3, p4[0], *w_down)
    activate(g4, h4)
    s4 = down_of(4, None, [])
    plus = moved(s4, 0, 1)
    a3 = activate(g3, h3, s4)
    h2 = sent_out(p2, a3)
    r3 = down_of(-3, None, [])
    minus = moved(r3, 0, -1)
    h1 = sent_out(p1, r3)
    s3 = down_of(3, None, [plus], r3)
    plus = moved(s3, 0, 1)
    a2 = activate(g2, h2, r3)
    activate(g1, h1, a2)
    plus = moved(down_of(2, None, [plus]), 0, 1)
    minus = moved(down_of(-2, None, [minus]), 0, -1)
    plus = [moved(down_of(1, c, [plus]), 0, 1) for c in (0, 1)]
    minus = [moved(down_of(-1, c, [minus]), 0, -1) for c in (0, 1)]
    halves = [down_of(0, c, [plus[c], minus[c]]) for c in (0, 1)]

    def gathered(home):
        def rows_for(d):
            return lax.dynamic_index_in_dim(home, place(d), 0, keepdims=False)

        there = [rows_for(0)] + [moved(rows_for(NY - s), -s, 0) for s in range(1, NY)]
        return jnp.roll(jnp.stack(there), y, axis=0)

    routed = [gathered(h.reshape(NY, tokens, part // 2)) for h in halves]
    routed = jnp.concatenate(routed, axis=2).transpose(1, 0, 2).reshape(tokens, width)
    mixed = (arrived.astype(F32) + routed.astype(F32)).astype(BF16)
    return mixed[None]


def solution(mesh):
    in_specs = (
        P("section", "expert", None),
        P("section", None),
        P("section", None, "expert"),
        P("section", None, "expert"),
        P("section", "expert", None),
        P("section", "expert", None),
        P("section", "expert", None),
    )
    out_specs = P("section", "expert", None)
    return jax.shard_map(
        per_device, mesh=mesh, in_specs=in_specs, out_specs=out_specs, check_vma=False
    )
```

```python
import functools

import jax
import jax.numpy as jnp
from jax import lax
from jax.experimental import pallas as pl
from jax.experimental.pallas import tpu as pltpu
from jax.sharding import PartitionSpec as P

ROUTE_SCALE = 2.5
EPSILON = 1e-06
NY = 4
NZ = 8
SLICES = 4
LANES = 128
BF16 = jnp.bfloat16
F32 = jnp.float32
VMEM_BYTES = 48 * 1024 * 1024
LITTLE = pl.CostEstimate(flops=1024, bytes_accessed=1024, transcendentals=0)


def moved(x, dy, dz):
    sections = lax.axis_size("section")
    pairs = []
    for s in range(sections):
        sign = 1 if s % 2 == 0 else -1
        for y in range(NY):
            for z in range(NZ):
                to = ((y + sign * dy) % NY) * NZ + (z + sign * dz) % NZ
                pairs.append((s * NY * NZ + y * NZ + z, s * NY * NZ + to))
    return lax.ppermute(x, ("section", "expert"), pairs)


def next_section(x, dy=0):
    sections = lax.axis_size("section")
    pairs = []
    for s in range(sections):
        to_section = (s + 1) % sections
        sign = 1 if to_section % 2 == 0 else -1
        for y in range(NY):
            for z in range(NZ):
                to = ((y + sign * dy) % NY) * NZ + z
                pairs.append((s * NY * NZ + y * NZ + z, to_section * NY * NZ + to))
    return lax.ppermute(x, ("section", "expert"), pairs)


def three_parts(x):
    high = lax.reduce_precision(x, 8, 7)
    middle = lax.reduce_precision(x - high, 8, 7)
    return [high, middle, x - high - middle]


def route_weights(scores):
    gate_values = jax.nn.sigmoid(scores)
    return ROUTE_SCALE * gate_values / jnp.sum(gate_values, axis=-1, keepdims=True)


def dot(a, b):
    return jnp.dot(a, b, preferred_element_type=F32)


def after(x, *others):
    return lax.optimization_barrier((x, *others))[0]


def route_lanes(routes, logits, experts):
    hits = routes[:, :, None] == jnp.arange(experts, dtype=jnp.int32)
    weight = jnp.sum(hits.astype(F32) * route_weights(logits)[:, :, None], axis=1)
    named = jnp.sum(hits.astype(jnp.int32), axis=1)
    slot = jnp.where(named > 0, jnp.cumsum(named, axis=0) - 1, -1).astype(F32)
    parts = jnp.concatenate(three_parts(weight) + [slot], axis=1).astype(BF16)
    return jnp.pad(parts, ((0, 0), (0, LANES - parts.shape[1])))


def lane_choice(columns, experts):
    lane = jnp.arange(LANES, dtype=jnp.int32)[None, :]
    expert = columns[:, None]
    weight = (lane == expert) | (lane == experts + expert) | (lane == 2 * experts + expert)
    slot = lane == 3 * experts + expert
    rows = jnp.concatenate([weight, slot], axis=0).astype(BF16)
    return jnp.pad(rows, ((0, LANES - rows.shape[0]), (0, 0)))


def quarter_kernel(place_ref, x_ref, *out_refs):
    tokens, width = x_ref.shape
    part = width // NY
    widened = x_ref[...].astype(F32)
    mean = jnp.sum(widened * widened, axis=-1, keepdims=True) * (1.0 / width)
    factor = lax.rsqrt(mean + EPSILON)
    high = factor.astype(BF16).astype(F32)
    middle = (factor - high).astype(BF16).astype(F32)
    low = factor - high - middle
    lane = lax.broadcasted_iota(jnp.int32, (tokens, LANES), 1)
    lanes = jnp.where(lane == 0, high, jnp.where(lane == 1, middle, jnp.where(lane == 2, low, 0.0)))
    for s, out_ref in enumerate(out_refs):
        first = pl.multiple_of(place_ref[s] * part, LANES)
        out_ref[:, :part] = x_ref[:, pl.ds(first, part)]
        out_ref[:, part:] = lanes.astype(BF16)


def quarters_of(rows, places):
    tokens, width = rows.shape
    spec = pl.BlockSpec(memory_space=pltpu.VMEM)
    shape = jax.ShapeDtypeStruct((tokens, width // NY + LANES), BF16)
    return pl.pallas_call(
        quarter_kernel,
        out_shape=[shape] * NY,
        in_specs=[pl.BlockSpec(memory_space=pltpu.SMEM), spec],
        out_specs=[spec] * NY,
        compiler_params=pltpu.CompilerParams(vmem_limit_bytes=VMEM_BYTES),
        cost_estimate=LITTLE,
    )(places, rows)


def block_kernel(part, y_ref, gain_ref, *refs):
    out_ref = refs[-1]
    tokens = refs[0].shape[0]
    for s in range(NY):
        row_ref, lane_ref = refs[s], refs[NY + s]
        home = pl.multiple_of(lax.rem(y_ref[0] + s, NY) * tokens, tokens)
        factor = row_ref[:, part:].astype(F32)
        factor = factor[:, :1] + factor[:, 1:2] + factor[:, 2:3]
        rows = row_ref[:, :part].astype(F32) * factor * gain_ref[...]
        out_ref[pl.ds(home, tokens), :part] = rows.astype(BF16)
        out_ref[pl.ds(home, tokens), part:] = lane_ref[...]


def normed_block(y, gain, rows, lanes):
    tokens, columns = rows[0].shape
    spec = pl.BlockSpec(memory_space=pltpu.VMEM)
    return pl.pallas_call(
        functools.partial(block_kernel, columns - LANES),
        out_shape=jax.ShapeDtypeStruct((NY * tokens, columns), BF16),
        in_specs=[pl.BlockSpec(memory_space=pltpu.SMEM)] + [spec] * (1 + 2 * NY),
        out_specs=spec,
        compiler_params=pltpu.CompilerParams(vmem_limit_bytes=VMEM_BYTES),
        cost_estimate=LITTLE,
    )(y.reshape(1).astype(jnp.int32), gain, *rows, *lanes)


def hidden_kernel(blocks, part, tokens, seats, devices, *refs):
    x_refs, choice_ref = refs[:blocks], refs[blocks]
    count = len(devices)
    w_refs = refs[blocks + 1 : blocks + 1 + count]
    out_refs = refs[blocks + 1 + count : blocks + 1 + 2 * count]
    picked_ref = refs[-1]
    rows = NY * tokens
    slots = NY * seats
    hid = w_refs[0].shape[1] // 2
    choice = choice_ref[...]
    number = lax.broadcasted_iota(jnp.int32, (slots, rows), 0)
    first = lax.broadcasted_iota(jnp.int32, (1, rows), 1) // tokens * seats
    for s, w_ref, out_ref in zip(devices, w_refs, out_refs):
        for b in range(blocks):
            info = lax.dot_general(
                choice,
                x_refs[b][:, part:],
                (((1,), (1,)), ((), ())),
                preferred_element_type=F32,
            )
            slot = info[NY + s : NY + s + 1, :].astype(jnp.int32)
            code = jnp.where(slot < 0, -1, slot + first)
            select = (number == code).astype(F32).astype(BF16)
            picked_ref[b * slots : (b + 1) * slots, :] = dot(select, x_refs[b][...]).astype(BF16)
        info = lax.dot_general(
            picked_ref[:, part:], choice, (((1,), (1,)), ((), ())), preferred_element_type=F32
        )
        sums = dot(picked_ref[:, :part], w_ref[...])
        out_ref[:, :hid] = sums[:, :hid].astype(out_ref.dtype)
        out_ref[:, hid:] = (sums[:, hid:] * info[:, s : s + 1]).astype(out_ref.dtype)


def hidden_partials(rows, choice, weights, devices, tokens, seats):
    blocks = len(rows)
    part, hid2 = weights[devices[0]].shape
    slots = NY * seats
    spec = pl.BlockSpec(memory_space=pltpu.VMEM)
    shape = (blocks * slots, hid2)
    count = len(devices)
    return pl.pallas_call(
        functools.partial(hidden_kernel, blocks, part, tokens, seats, devices),
        out_shape=[jax.ShapeDtypeStruct(shape, F32 if s == 0 else BF16) for s in devices],
        in_specs=[spec] * (blocks + 1 + count),
        out_specs=[spec] * count,
        scratch_shapes=[pltpu.VMEM((blocks * slots, part + LANES), BF16)],
        compiler_params=pltpu.CompilerParams(vmem_limit_bytes=VMEM_BYTES),
        cost_estimate=LITTLE,
    )(*rows, choice, *[weights[s] for s in devices])


def down_kernel(part, tokens, seats, arriving, *refs):
    x_ref, choice_ref = refs[:2]
    act_refs = refs[2 : 2 + NY]
    w_refs = refs[2 + NY : 2 + 2 * NY]
    sent_refs = refs[2 + 2 * NY : 2 + 2 * NY + arriving]
    out_ref = refs[-2]
    wide_ref = refs[-1]
    rows = NY * tokens
    slots = NY * seats
    hid = act_refs[0].shape[1]
    info = lax.dot_general(
        x_ref[...], choice_ref[...], (((1,), (1,)), ((), ())), preferred_element_type=F32
    )
    number = lax.broadcasted_iota(jnp.int32, (rows, slots), 1)
    first = lax.broadcasted_iota(jnp.int32, (rows, 1), 0) // tokens * seats
    for s in range(NY):
        slot = info[:, NY + s : NY + s + 1].astype(jnp.int32)
        code = jnp.where(slot < 0, -1, slot + first)
        select = (number == code).astype(F32).astype(BF16)
        wide_ref[:, s * hid : (s + 1) * hid] = dot(select, act_refs[s][...]).astype(BF16)
    wide = out_ref.shape[1]
    for c in range(0, wide, 256):
        columns = slice(c, min(c + 256, wide))
        total = dot(wide_ref[:, :hid], w_refs[0][:, columns])
        for s in range(1, NY):
            total += dot(wide_ref[:, s * hid : (s + 1) * hid], w_refs[s][:, columns])
        for sent in sent_refs:
            total += sent[:, columns].astype(F32)
        out_ref[:, columns] = total.astype(BF16)


def columns_of(rows, wide, at):
    return pl.BlockSpec((rows, wide), lambda i: (0, at))


def down_sums(block, choice, acts, weights, half, sent, tokens, seats):
    hid, part = weights[0].shape
    rows = NY * tokens
    wide, at = (part, 0) if half is None else (part // 2, half)
    spec = pl.BlockSpec(memory_space=pltpu.VMEM)
    lanes = pl.BlockSpec((rows, LANES), lambda i: (0, part // LANES))
    columns = columns_of(hid, wide, at)
    there = [columns_of(rows, wide, at if r.shape[1] == part else 0) for r in sent]
    return pl.pallas_call(
        functools.partial(down_kernel, part, tokens, seats, len(sent)),
        out_shape=jax.ShapeDtypeStruct((rows, wide), BF16),
        grid=(1,),
        in_specs=[lanes] + [spec] * (1 + NY) + [columns] * NY + there,
        out_specs=spec,
        scratch_shapes=[pltpu.VMEM((rows, NY * hid), BF16)],
        compiler_params=pltpu.CompilerParams(vmem_limit_bytes=VMEM_BYTES),
        cost_estimate=LITTLE,
    )(block, choice, *acts, *weights, *sent)


def per_device(hidden, norm_gain, gate_weight, up_weight, down_weight, routes, logits):
    me = lax.axis_index("expert")
    odd = lax.axis_index("section") % 2
    y = jnp.where(odd == 1, (NY - me // NZ) % NY, me // NZ)
    tokens, width = hidden.shape[1], hidden.shape[2]
    top = routes.shape[2]
    hid = gate_weight.shape[2]
    part = width // NY
    experts = lax.axis_size("expert") // SLICES
    seats = 2 * tokens * top // experts
    gate, up, down = gate_weight[0], up_weight[0], down_weight[0]

    def place(d):
        return (y + d) % NY

    there_y = (NY - y) % NY
    places = (there_y + NY - jnp.arange(NY, dtype=jnp.int32)) % NY
    outgoing = quarters_of(hidden[0], places.astype(jnp.int32))
    rows = [next_section(r, (NY - s) % NY) for s, r in enumerate(outgoing)]
    lanes = route_lanes(*lax.optimization_barrier((routes[0], logits[0], outgoing[0]))[:2], experts)
    there = (jnp.arange(NY, dtype=jnp.int32) * jnp.where(odd == 1, -1, 1) + me // NZ) % NY
    choice = lane_choice(there * (NZ // SLICES) + me % NZ // SLICES, experts)
    homes = [lanes] + [moved(lanes, NY - s, 0) for s in range(1, NY)]
    gain = lax.dynamic_slice(norm_gain, (0, y * part), (1, part))
    block = normed_block(y, gain, rows, homes)
    arrived = next_section(hidden[0])

    def gate_up_for(d, *earlier):
        start = (after(place(d), *earlier) * part, 0)
        return jnp.concatenate(
            [lax.dynamic_slice(w, start, (part, hid)) for w in (gate, up)], axis=1
        )

    def down_for(d, *earlier):
        return lax.dynamic_slice(down, (0, after(place(d), *earlier) * part), (hid, part))

    x = {0: block}

    def step(k, forth, back):
        x[k] = moved(forth, 0, -1)
        if k < NZ // 2:
            x[-k] = moved(back, 0, 1)

    barrier = lax.optimization_barrier
    far, forth = barrier((gate_up_for(2, *homes[1:]), block))
    w_in = {2: moved(far, 2, 0)}
    step(1, forth, forth)
    step(2, x[1], x[-1])
    w_in[0], w_down = gate_up_for(0, x[1]), [down_for(0, x[1])]
    left, near, forth, back, w_in[2], arrived = barrier(
        (gate_up_for(3, x[1]), gate_up_for(1, x[1]), x[2], x[-2], w_in[2], arrived)
    )
    w_in[1], w_in[3] = moved(left, -1, 0), moved(near, 1, 0)
    step(3, forth, back)

    slots = NY * seats
    acts = {}

    def partials(keys, devices, *earlier):
        rows = [after(x[k], *earlier) for k in keys]
        return dict(zip(devices, hidden_partials(rows, choice, w_in, devices, tokens, seats)))

    def sent_out(sums, *earlier):
        return [sums[0]] + [moved(after(sums[s], *earlier), s, 0) for s in (1, 2, 3)]

    def activate(keys, sums, *earlier):
        total = after(sums[0], *earlier)
        for r in sums[1:]:
            total = total + r.astype(F32)
        act = (jax.nn.silu(total[:, :hid]) * total[:, hid:]).astype(BF16)
        everyone = [act] + [moved(act, -s, 0) for s in range(1, NY)]
        for i, k in enumerate(keys):
            acts[k] = (everyone, i)
        return act

    def down_of(k, half, sent, *earlier):
        group, at = acts[k]
        group = [after(group[0], *earlier)] + group[1:]
        block_acts = [a[at * slots : (at + 1) * slots] for a in group]
        return down_sums(x[k], choice, block_acts, w_down, half, sent, tokens, seats)

    g4, g3, g2, g1 = (4,), (3, -3), (2, -2), (1, -1, 0)
    p1, p2 = (partials(g, (0, 2)) for g in (g1, g2))
    downs = [down_for(NY - s, x[2]) for s in (1, 2, 3)]
    forth, downs, w_in[1], w_in[3], *_ = barrier(
        (x[3], downs, w_in[1], w_in[3], p1[0], p2[0])
    )
    step(4, forth, None)
    w_down += [moved(w, -s, 0) for s, w in enumerate(downs, 1)]
    p3 = partials(g3, (2, 1, 3, 0))
    p2.update(partials(g2, (1, 3), p3[0]))
    p1.update(partials(g1, (1, 3), p2[1]))
    p4 = partials(g4, (2, 1, 3, 0), p1[1])
    h4 = sent_out(p4, *w_down)
    activate(g4, h4)
    h3 = sent_out(p3, *acts[4][0][1:])
    s4 = down_of(4, None, [])
    plus = moved(s4, 0, 1)
    a3 = activate(g3, h3, s4)
    h2 = sent_out(p2, a3)
    r3 = down_of(-3, None, [])
    minus = moved(r3, 0, -1)
    s3 = down_of(3, None, [plus], r3)
    plus = moved(s3, 0, 1)
    a2 = activate(g2, h2, s3)
    h1 = sent_out(p1, a2)
    s2, r2 = down_of(2, None, [plus]), down_of(-2, None, [minus])
    plus, minus = moved(s2, 0, 1), moved(r2, 0, -1)
    activate(g1, h1, s2, r2)
    plus = [moved(down_of(1, c, [plus]), 0, 1) for c in (0, 1)]
    minus = [moved(down_of(-1, c, [minus]), 0, -1) for c in (0, 1)]
    halves = [down_of(0, c, [plus[c], minus[c]]) for c in (0, 1)]

    def gathered(home):
        def rows_for(d):
            return lax.dynamic_index_in_dim(home, place(d), 0, keepdims=False)

        there = [rows_for(0)] + [moved(rows_for(NY - s), -s, 0) for s in range(1, NY)]
        return jnp.roll(jnp.stack(there), y, axis=0)

    routed = [gathered(h.reshape(NY, tokens, part // 2)) for h in halves]
    routed = jnp.concatenate(routed, axis=2).transpose(1, 0, 2).reshape(tokens, width)
    mixed = (arrived.astype(F32) + routed.astype(F32)).astype(BF16)
    return mixed[None]


def solution(mesh):
    in_specs = (
        P("section", "expert", None),
        P("section", None),
        P("section", None, "expert"),
        P("section", None, "expert"),
        P("section", "expert", None),
        P("section", "expert", None),
        P("section", "expert", None),
    )
    out_specs = P("section", "expert", None)
    return jax.shard_map(
        per_device, mesh=mesh, in_specs=in_specs, out_specs=out_specs, check_vma=False
    )
```

```python
import functools

import jax
import jax.numpy as jnp
from jax import lax
from jax.experimental import pallas as pl
from jax.experimental.pallas import tpu as pltpu
from jax.sharding import PartitionSpec as P

ROUTE_SCALE = 2.5
EPSILON = 1e-06
NY = 4
NZ = 8
SLICES = 4
LANES = 128
BF16 = jnp.bfloat16
F32 = jnp.float32
VMEM_BYTES = 48 * 1024 * 1024
LITTLE = pl.CostEstimate(flops=1024, bytes_accessed=1024, transcendentals=0)


def moved(x, dy, dz):
    sections = lax.axis_size("section")
    pairs = []
    for s in range(sections):
        sign = 1 if s % 2 == 0 else -1
        for y in range(NY):
            for z in range(NZ):
                to = ((y + sign * dy) % NY) * NZ + (z + sign * dz) % NZ
                pairs.append((s * NY * NZ + y * NZ + z, s * NY * NZ + to))
    return lax.ppermute(x, ("section", "expert"), pairs)


def next_section(x, dy=0):
    sections = lax.axis_size("section")
    pairs = []
    for s in range(sections):
        to_section = (s + 1) % sections
        sign = 1 if to_section % 2 == 0 else -1
        for y in range(NY):
            for z in range(NZ):
                to = ((y + sign * dy) % NY) * NZ + z
                pairs.append((s * NY * NZ + y * NZ + z, to_section * NY * NZ + to))
    return lax.ppermute(x, ("section", "expert"), pairs)


def three_parts(x):
    high = lax.reduce_precision(x, 8, 7)
    middle = lax.reduce_precision(x - high, 8, 7)
    return [high, middle, x - high - middle]


def route_weights(scores):
    gate_values = jax.nn.sigmoid(scores)
    return ROUTE_SCALE * gate_values / jnp.sum(gate_values, axis=-1, keepdims=True)


def dot(a, b):
    return jnp.dot(a, b, preferred_element_type=F32)


def after(x, *others):
    return lax.optimization_barrier((x, *others))[0]


def route_lanes(routes, logits, experts):
    hits = routes[:, :, None] == jnp.arange(experts, dtype=jnp.int32)
    weight = jnp.sum(hits.astype(F32) * route_weights(logits)[:, :, None], axis=1)
    named = jnp.sum(hits.astype(jnp.int32), axis=1)
    slot = jnp.where(named > 0, jnp.cumsum(named, axis=0) - 1, -1).astype(F32)
    parts = jnp.concatenate(three_parts(weight) + [slot], axis=1).astype(BF16)
    return jnp.pad(parts, ((0, 0), (0, LANES - parts.shape[1])))


def lane_choice(columns, experts):
    lane = jnp.arange(LANES, dtype=jnp.int32)[None, :]
    expert = columns[:, None]
    weight = (lane == expert) | (lane == experts + expert) | (lane == 2 * experts + expert)
    slot = lane == 3 * experts + expert
    rows = jnp.concatenate([weight, slot], axis=0).astype(BF16)
    return jnp.pad(rows, ((0, LANES - rows.shape[0]), (0, 0)))


def quarter_kernel(place_ref, x_ref, *out_refs):
    tokens, width = x_ref.shape
    part = width // NY
    widened = x_ref[...].astype(F32)
    mean = jnp.sum(widened * widened, axis=-1, keepdims=True) * (1.0 / width)
    factor = lax.rsqrt(mean + EPSILON)
    high = factor.astype(BF16).astype(F32)
    middle = (factor - high).astype(BF16).astype(F32)
    low = factor - high - middle
    lane = lax.broadcasted_iota(jnp.int32, (tokens, LANES), 1)
    lanes = jnp.where(lane == 0, high, jnp.where(lane == 1, middle, jnp.where(lane == 2, low, 0.0)))
    for s, out_ref in enumerate(out_refs):
        first = pl.multiple_of(place_ref[s] * part, LANES)
        out_ref[:, :part] = x_ref[:, pl.ds(first, part)]
        out_ref[:, part:] = lanes.astype(BF16)


def quarters_of(rows, places):
    tokens, width = rows.shape
    spec = pl.BlockSpec(memory_space=pltpu.VMEM)
    shape = jax.ShapeDtypeStruct((tokens, width // NY + LANES), BF16)
    return pl.pallas_call(
        quarter_kernel,
        out_shape=[shape] * NY,
        in_specs=[pl.BlockSpec(memory_space=pltpu.SMEM), spec],
        out_specs=[spec] * NY,
        compiler_params=pltpu.CompilerParams(vmem_limit_bytes=VMEM_BYTES),
        cost_estimate=LITTLE,
    )(places, rows)


def block_kernel(part, y_ref, gain_ref, *refs):
    out_ref = refs[-1]
    tokens = refs[0].shape[0]
    for s in range(NY):
        row_ref, lane_ref = refs[s], refs[NY + s]
        home = pl.multiple_of(lax.rem(y_ref[0] + s, NY) * tokens, tokens)
        factor = row_ref[:, part:].astype(F32)
        factor = factor[:, :1] + factor[:, 1:2] + factor[:, 2:3]
        rows = row_ref[:, :part].astype(F32) * factor * gain_ref[...]
        out_ref[pl.ds(home, tokens), :part] = rows.astype(BF16)
        out_ref[pl.ds(home, tokens), part:] = lane_ref[...]


def normed_block(y, gain, rows, lanes):
    tokens, columns = rows[0].shape
    spec = pl.BlockSpec(memory_space=pltpu.VMEM)
    return pl.pallas_call(
        functools.partial(block_kernel, columns - LANES),
        out_shape=jax.ShapeDtypeStruct((NY * tokens, columns), BF16),
        in_specs=[pl.BlockSpec(memory_space=pltpu.SMEM)] + [spec] * (1 + 2 * NY),
        out_specs=spec,
        compiler_params=pltpu.CompilerParams(vmem_limit_bytes=VMEM_BYTES),
        cost_estimate=LITTLE,
    )(y.reshape(1).astype(jnp.int32), gain, *rows, *lanes)


def hidden_kernel(blocks, part, tokens, seats, devices, *refs):
    x_refs, choice_ref = refs[:blocks], refs[blocks]
    count = len(devices)
    w_refs = refs[blocks + 1 : blocks + 1 + count]
    out_refs = refs[blocks + 1 + count : blocks + 1 + 2 * count]
    picked_ref = refs[-1]
    rows = NY * tokens
    slots = NY * seats
    hid = w_refs[0].shape[1] // 2
    choice = choice_ref[...]
    number = lax.broadcasted_iota(jnp.int32, (slots, rows), 0)
    first = lax.broadcasted_iota(jnp.int32, (1, rows), 1) // tokens * seats
    for s, w_ref, out_ref in zip(devices, w_refs, out_refs):
        for b in range(blocks):
            info = lax.dot_general(
                choice,
                x_refs[b][:, part:],
                (((1,), (1,)), ((), ())),
                preferred_element_type=F32,
            )
            slot = info[NY + s : NY + s + 1, :].astype(jnp.int32)
            code = jnp.where(slot < 0, -1, slot + first)
            select = (number == code).astype(F32).astype(BF16)
            picked_ref[b * slots : (b + 1) * slots, :] = dot(select, x_refs[b][...]).astype(BF16)
        info = lax.dot_general(
            picked_ref[:, part:], choice, (((1,), (1,)), ((), ())), preferred_element_type=F32
        )
        sums = dot(picked_ref[:, :part], w_ref[...])
        out_ref[:, :hid] = sums[:, :hid].astype(out_ref.dtype)
        out_ref[:, hid:] = (sums[:, hid:] * info[:, s : s + 1]).astype(out_ref.dtype)


def hidden_partials(rows, choice, weights, devices, tokens, seats):
    blocks = len(rows)
    part, hid2 = weights[devices[0]].shape
    slots = NY * seats
    spec = pl.BlockSpec(memory_space=pltpu.VMEM)
    shape = (blocks * slots, hid2)
    count = len(devices)
    return pl.pallas_call(
        functools.partial(hidden_kernel, blocks, part, tokens, seats, devices),
        out_shape=[jax.ShapeDtypeStruct(shape, F32 if s == 0 else BF16) for s in devices],
        in_specs=[spec] * (blocks + 1 + count),
        out_specs=[spec] * count,
        scratch_shapes=[pltpu.VMEM((blocks * slots, part + LANES), BF16)],
        compiler_params=pltpu.CompilerParams(vmem_limit_bytes=VMEM_BYTES),
        cost_estimate=LITTLE,
    )(*rows, choice, *[weights[s] for s in devices])


def down_kernel(part, tokens, seats, arriving, *refs):
    x_ref, choice_ref = refs[:2]
    act_refs = refs[2 : 2 + NY]
    w_refs = refs[2 + NY : 2 + 2 * NY]
    sent_refs = refs[2 + 2 * NY : 2 + 2 * NY + arriving]
    out_refs, wide_ref = refs[2 + 2 * NY + arriving : -1], refs[-1]
    rows = NY * tokens
    slots = NY * seats
    hid = act_refs[0].shape[1]
    info = lax.dot_general(
        x_ref[...], choice_ref[...], (((1,), (1,)), ((), ())), preferred_element_type=F32
    )
    number = lax.broadcasted_iota(jnp.int32, (rows, slots), 1)
    first = lax.broadcasted_iota(jnp.int32, (rows, 1), 0) // tokens * seats
    for s in range(NY):
        slot = info[:, NY + s : NY + s + 1].astype(jnp.int32)
        code = jnp.where(slot < 0, -1, slot + first)
        select = (number == code).astype(F32).astype(BF16)
        wide_ref[:, s * hid : (s + 1) * hid] = dot(select, act_refs[s][...]).astype(BF16)
    wide = out_refs[0].shape[1]
    for number, out_ref in enumerate(out_refs):
        for c in range(0, wide, 256):
            end = min(c + 256, wide)
            columns = slice(number * wide + c, number * wide + end)
            total = dot(wide_ref[:, :hid], w_refs[0][:, columns])
            for s in range(1, NY):
                total += dot(wide_ref[:, s * hid : (s + 1) * hid], w_refs[s][:, columns])
            for sent in sent_refs:
                total += sent[:, columns].astype(F32)
            out_ref[:, c:end] = total.astype(BF16)


def columns_of(rows, wide, at):
    return pl.BlockSpec((rows, wide), lambda i: (0, at))


def down_sums(block, choice, acts, weights, half, sent, tokens, seats):
    hid, part = weights[0].shape
    rows = NY * tokens
    wide, at = (part // 2, half) if half in (0, 1) else (part, 0)
    shape = jax.ShapeDtypeStruct((rows, part if half is None else part // 2), BF16)
    spec = pl.BlockSpec(memory_space=pltpu.VMEM)
    lanes = pl.BlockSpec((rows, LANES), lambda i: (0, part // LANES))
    columns = columns_of(hid, wide, at)
    there = [columns_of(rows, wide, at if r.shape[1] == part else 0) for r in sent]
    return pl.pallas_call(
        functools.partial(down_kernel, part, tokens, seats, len(sent)),
        out_shape=[shape] * (2 if half == 2 else 1),
        grid=(1,),
        in_specs=[lanes] + [spec] * (1 + NY) + [columns] * NY + there,
        out_specs=[spec] * (2 if half == 2 else 1),
        scratch_shapes=[pltpu.VMEM((rows, NY * hid), BF16)],
        compiler_params=pltpu.CompilerParams(vmem_limit_bytes=VMEM_BYTES),
        cost_estimate=LITTLE,
    )(block, choice, *acts, *weights, *sent)


def per_device(hidden, norm_gain, gate_weight, up_weight, down_weight, routes, logits):
    me = lax.axis_index("expert")
    odd = lax.axis_index("section") % 2
    y = jnp.where(odd == 1, (NY - me // NZ) % NY, me // NZ)
    tokens, width = hidden.shape[1], hidden.shape[2]
    top = routes.shape[2]
    hid = gate_weight.shape[2]
    part = width // NY
    experts = lax.axis_size("expert") // SLICES
    seats = 2 * tokens * top // experts
    gate, up, down = gate_weight[0], up_weight[0], down_weight[0]

    def place(d):
        return (y + d) % NY

    def gate_up_for(d, *earlier):
        at = after(place(d), *earlier) if earlier else place(d)
        start = (at * part, 0)
        return jnp.concatenate(
            [lax.dynamic_slice(w, start, (part, hid)) for w in (gate, up)], axis=1
        )

    def down_for(d, *earlier):
        return lax.dynamic_slice(down, (0, after(place(d), *earlier) * part), (hid, part))

    there_y = (NY - y) % NY
    places = (there_y + NY - jnp.arange(NY, dtype=jnp.int32)) % NY
    outgoing = quarters_of(hidden[0], places.astype(jnp.int32))
    rows = [next_section(r, (NY - s) % NY) for s, r in enumerate(outgoing)]
    lanes = route_lanes(*lax.optimization_barrier((routes[0], logits[0], rows[0]))[:2], experts)
    there = (jnp.arange(NY, dtype=jnp.int32) * jnp.where(odd == 1, -1, 1) + me // NZ) % NY
    choice = lane_choice(there * (NZ // SLICES) + me % NZ // SLICES, experts)
    homes = [lanes] + [moved(lanes, NY - s, 0) for s in range(1, NY)]
    gain = lax.dynamic_slice(norm_gain, (0, y * part), (1, part))
    block = normed_block(y, gain, rows, homes)
    arrived = next_section(hidden[0])

    x = {0: block}

    def step(k, forth, back):
        x[k] = moved(forth, 0, -1)
        if k < NZ // 2:
            x[-k] = moved(back, 0, 1)

    barrier = lax.optimization_barrier
    far, forth = barrier((gate_up_for(2, rows[0]), block))
    w_in = {2: moved(far, 2, 0)}
    step(1, forth, forth)
    step(2, x[1], x[-1])
    w_in[0], w_down = gate_up_for(0, x[1]), [down_for(0, x[1])]
    left, near, forth, back, w_in[2], arrived = barrier(
        (gate_up_for(3, x[1]), gate_up_for(1, x[1]), x[2], x[-2], w_in[2], arrived)
    )
    w_in[1], w_in[3] = moved(left, -1, 0), moved(near, 1, 0)
    step(3, forth, back)

    slots = NY * seats
    acts = {}

    def partials(keys, devices, *earlier):
        rows = [after(x[k], *earlier) for k in keys]
        return dict(zip(devices, hidden_partials(rows, choice, w_in, devices, tokens, seats)))

    def sent_out(sums, *earlier):
        return [sums[0]] + [moved(after(sums[s], *earlier), s, 0) for s in (1, 2, 3)]

    def activate(keys, sums, *earlier):
        total = after(sums[0], *earlier)
        for r in sums[1:]:
            total = total + r.astype(F32)
        act = (jax.nn.silu(total[:, :hid]) * total[:, hid:]).astype(BF16)
        everyone = [act] + [moved(act, -s, 0) for s in range(1, NY)]
        for i, k in enumerate(keys):
            acts[k] = (everyone, i)
        return act

    def down_of(k, half, sent, *earlier):
        group, at = acts[k]
        group = [after(group[0], *earlier)] + group[1:]
        block_acts = [a[at * slots : (at + 1) * slots] for a in group]
        sums = down_sums(x[k], choice, block_acts, w_down, half, sent, tokens, seats)
        return sums if half == 2 else sums[0]

    g4, g3, g2, g1 = (4,), (3, -3), (2, -2), (1, -1, 0)
    p1, p2 = (partials(g, (0, 2)) for g in (g1, g2))
    downs = [down_for(NY - s, x[2]) for s in (1, 2, 3)]
    forth, downs, w_in[1], w_in[3], *_ = barrier(
        (x[3], downs, w_in[1], w_in[3], p1[0], p2[0])
    )
    step(4, forth, None)
    w_down += [moved(w, -s, 0) for s, w in enumerate(downs, 1)]
    p3 = partials(g3, (2, 1, 3, 0))
    p2.update(partials(g2, (1, 3), p3[0]))
    p1.update(partials(g1, (1, 3), p2[1]))
    p4 = partials(g4, (2, 1, 3, 0), p1[1])
    h4 = sent_out(p4, *w_down)
    activate(g4, h4)
    h3 = sent_out(p3, *acts[4][0][1:])
    s4 = down_of(4, None, [])
    plus = moved(s4, 0, 1)
    a3 = activate(g3, h3, s4)
    h2 = sent_out(p2, a3)
    r3 = down_of(-3, None, [])
    minus = moved(r3, 0, -1)
    s3 = down_of(3, None, [plus], r3)
    plus = moved(s3, 0, 1)
    a2 = activate(g2, h2, s3)
    h1 = sent_out(p1, a2)
    s2, r2 = down_of(2, None, [plus]), down_of(-2, None, [minus])
    plus, minus = moved(s2, 0, 1), moved(r2, 0, -1)
    activate(g1, h1, s2, r2)
    plus = [moved(s, 0, 1) for s in down_of(1, 2, [plus])]
    minus = [moved(s, 0, -1) for s in down_of(-1, 2, [minus])]
    halves = [down_of(0, c, [plus[c], minus[c]]) for c in (0, 1)]

    def gathered(home):
        def rows_for(d):
            return lax.dynamic_index_in_dim(home, place(d), 0, keepdims=False)

        there = [rows_for(0)] + [moved(rows_for(NY - s), -s, 0) for s in range(1, NY)]
        return jnp.roll(jnp.stack(there), y, axis=0)

    routed = [gathered(h.reshape(NY, tokens, part // 2)) for h in halves]
    routed = jnp.concatenate(routed, axis=2).transpose(1, 0, 2).reshape(tokens, width)
    mixed = (arrived.astype(F32) + routed.astype(F32)).astype(BF16)
    return mixed[None]


def solution(mesh):
    in_specs = (
        P("section", "expert", None),
        P("section", None),
        P("section", None, "expert"),
        P("section", None, "expert"),
        P("section", "expert", None),
        P("section", "expert", None),
        P("section", "expert", None),
    )
    out_specs = P("section", "expert", None)
    return jax.shard_map(
        per_device, mesh=mesh, in_specs=in_specs, out_specs=out_specs, check_vma=False
    )
```

```python
import functools

import jax
import jax.numpy as jnp
from jax import lax
from jax.experimental import pallas as pl
from jax.experimental.pallas import tpu as pltpu
from jax.sharding import PartitionSpec as P

ROUTE_SCALE = 2.5
EPSILON = 1e-06
NY = 4
NZ = 8
SLICES = 4
LANES = 128
BF16 = jnp.bfloat16
F32 = jnp.float32
VMEM_BYTES = 48 * 1024 * 1024
LITTLE = pl.CostEstimate(flops=1024, bytes_accessed=1024, transcendentals=0)


def moved(x, dy, dz):
    sections = lax.axis_size("section")
    pairs = []
    for s in range(sections):
        sign = 1 if s % 2 == 0 else -1
        for y in range(NY):
            for z in range(NZ):
                to = ((y + sign * dy) % NY) * NZ + (z + sign * dz) % NZ
                pairs.append((s * NY * NZ + y * NZ + z, s * NY * NZ + to))
    return lax.ppermute(x, ("section", "expert"), pairs)


def next_section(x, dy=0):
    sections = lax.axis_size("section")
    pairs = []
    for s in range(sections):
        to_section = (s + 1) % sections
        sign = 1 if to_section % 2 == 0 else -1
        for y in range(NY):
            for z in range(NZ):
                to = ((y + sign * dy) % NY) * NZ + z
                pairs.append((s * NY * NZ + y * NZ + z, to_section * NY * NZ + to))
    return lax.ppermute(x, ("section", "expert"), pairs)


def three_parts(x):
    high = lax.reduce_precision(x, 8, 7)
    middle = lax.reduce_precision(x - high, 8, 7)
    return [high, middle, x - high - middle]


def route_weights(scores):
    gate_values = jax.nn.sigmoid(scores)
    return ROUTE_SCALE * gate_values / jnp.sum(gate_values, axis=-1, keepdims=True)


def dot(a, b):
    return jnp.dot(a, b, preferred_element_type=F32)


def after(x, *others):
    return lax.optimization_barrier((x, *others))[0]


def route_lanes(routes, logits, experts):
    hits = routes[:, :, None] == jnp.arange(experts, dtype=jnp.int32)
    weight = jnp.sum(hits.astype(F32) * route_weights(logits)[:, :, None], axis=1)
    named = jnp.sum(hits.astype(jnp.int32), axis=1)
    slot = jnp.where(named > 0, jnp.cumsum(named, axis=0) - 1, -1).astype(F32)
    parts = jnp.concatenate(three_parts(weight) + [slot], axis=1).astype(BF16)
    return jnp.pad(parts, ((0, 0), (0, LANES - parts.shape[1])))


def lane_choice(columns, experts):
    lane = jnp.arange(LANES, dtype=jnp.int32)[None, :]
    expert = columns[:, None]
    weight = (lane == expert) | (lane == experts + expert) | (lane == 2 * experts + expert)
    slot = lane == 3 * experts + expert
    rows = jnp.concatenate([weight, slot], axis=0).astype(BF16)
    return jnp.pad(rows, ((0, LANES - rows.shape[0]), (0, 0)))


def quarter_kernel(place_ref, x_ref, *out_refs):
    tokens, width = x_ref.shape
    part = width // NY
    widened = x_ref[...].astype(F32)
    mean = jnp.sum(widened * widened, axis=-1, keepdims=True) * (1.0 / width)
    factor = lax.rsqrt(mean + EPSILON)
    high = factor.astype(BF16).astype(F32)
    middle = (factor - high).astype(BF16).astype(F32)
    low = factor - high - middle
    lane = lax.broadcasted_iota(jnp.int32, (tokens, LANES), 1)
    lanes = jnp.where(lane == 0, high, jnp.where(lane == 1, middle, jnp.where(lane == 2, low, 0.0)))
    for s, out_ref in enumerate(out_refs):
        first = pl.multiple_of(place_ref[s] * part, LANES)
        out_ref[:, :part] = x_ref[:, pl.ds(first, part)]
        out_ref[:, part:] = lanes.astype(BF16)


def quarters_of(rows, places):
    tokens, width = rows.shape
    spec = pl.BlockSpec(memory_space=pltpu.VMEM)
    shape = jax.ShapeDtypeStruct((tokens, width // NY + LANES), BF16)
    return pl.pallas_call(
        quarter_kernel,
        out_shape=[shape] * NY,
        in_specs=[pl.BlockSpec(memory_space=pltpu.SMEM), spec],
        out_specs=[spec] * NY,
        compiler_params=pltpu.CompilerParams(vmem_limit_bytes=VMEM_BYTES),
        cost_estimate=LITTLE,
    )(places, rows)


def block_kernel(part, y_ref, gain_ref, *refs):
    out_ref = refs[-1]
    tokens = refs[0].shape[0]
    for s in range(NY):
        row_ref, lane_ref = refs[s], refs[NY + s]
        home = pl.multiple_of(lax.rem(y_ref[0] + s, NY) * tokens, tokens)
        factor = row_ref[:, part:].astype(F32)
        factor = factor[:, :1] + factor[:, 1:2] + factor[:, 2:3]
        rows = row_ref[:, :part].astype(F32) * factor * gain_ref[...]
        out_ref[pl.ds(home, tokens), :part] = rows.astype(BF16)
        out_ref[pl.ds(home, tokens), part:] = lane_ref[...]


def normed_block(y, gain, rows, lanes):
    tokens, columns = rows[0].shape
    spec = pl.BlockSpec(memory_space=pltpu.VMEM)
    return pl.pallas_call(
        functools.partial(block_kernel, columns - LANES),
        out_shape=jax.ShapeDtypeStruct((NY * tokens, columns), BF16),
        in_specs=[pl.BlockSpec(memory_space=pltpu.SMEM)] + [spec] * (1 + 2 * NY),
        out_specs=spec,
        compiler_params=pltpu.CompilerParams(vmem_limit_bytes=VMEM_BYTES),
        cost_estimate=LITTLE,
    )(y.reshape(1).astype(jnp.int32), gain, *rows, *lanes)


def hidden_kernel(blocks, part, tokens, seats, devices, *refs):
    x_refs, choice_ref = refs[:blocks], refs[blocks]
    count = len(devices)
    w_refs = refs[blocks + 1 : blocks + 1 + count]
    out_refs = refs[blocks + 1 + count : blocks + 1 + 2 * count]
    picked_ref = refs[-1]
    rows = NY * tokens
    slots = NY * seats
    hid = w_refs[0].shape[1] // 2
    choice = choice_ref[...]
    number = lax.broadcasted_iota(jnp.int32, (slots, rows), 0)
    first = lax.broadcasted_iota(jnp.int32, (1, rows), 1) // tokens * seats
    for s, w_ref, out_ref in zip(devices, w_refs, out_refs):
        for b in range(blocks):
            info = lax.dot_general(
                choice,
                x_refs[b][:, part:],
                (((1,), (1,)), ((), ())),
                preferred_element_type=F32,
            )
            slot = info[NY + s : NY + s + 1, :].astype(jnp.int32)
            code = jnp.where(slot < 0, -1, slot + first)
            select = (number == code).astype(F32).astype(BF16)
            picked_ref[b * slots : (b + 1) * slots, :] = dot(select, x_refs[b][...]).astype(BF16)
        info = lax.dot_general(
            picked_ref[:, part:], choice, (((1,), (1,)), ((), ())), preferred_element_type=F32
        )
        sums = dot(picked_ref[:, :part], w_ref[...])
        out_ref[:, :hid] = sums[:, :hid].astype(out_ref.dtype)
        out_ref[:, hid:] = (sums[:, hid:] * info[:, s : s + 1]).astype(out_ref.dtype)


def hidden_partials(rows, choice, weights, devices, tokens, seats):
    blocks = len(rows)
    part, hid2 = weights[devices[0]].shape
    slots = NY * seats
    spec = pl.BlockSpec(memory_space=pltpu.VMEM)
    shape = (blocks * slots, hid2)
    count = len(devices)
    return pl.pallas_call(
        functools.partial(hidden_kernel, blocks, part, tokens, seats, devices),
        out_shape=[jax.ShapeDtypeStruct(shape, F32 if s == 0 else BF16) for s in devices],
        in_specs=[spec] * (blocks + 1 + count),
        out_specs=[spec] * count,
        scratch_shapes=[pltpu.VMEM((blocks * slots, part + LANES), BF16)],
        compiler_params=pltpu.CompilerParams(vmem_limit_bytes=VMEM_BYTES),
        cost_estimate=LITTLE,
    )(*rows, choice, *[weights[s] for s in devices])


def down_kernel(part, tokens, seats, arriving, *refs):
    x_ref, choice_ref = refs[:2]
    act_refs = refs[2 : 2 + NY]
    w_refs = refs[2 + NY : 2 + 2 * NY]
    sent_refs = refs[2 + 2 * NY : 2 + 2 * NY + arriving]
    out_refs, wide_ref = refs[2 + 2 * NY + arriving : -1], refs[-1]
    rows = NY * tokens
    slots = NY * seats
    hid = act_refs[0].shape[1]
    info = lax.dot_general(
        x_ref[...], choice_ref[...], (((1,), (1,)), ((), ())), preferred_element_type=F32
    )
    number = lax.broadcasted_iota(jnp.int32, (rows, slots), 1)
    first = lax.broadcasted_iota(jnp.int32, (rows, 1), 0) // tokens * seats
    for s in range(NY):
        slot = info[:, NY + s : NY + s + 1].astype(jnp.int32)
        code = jnp.where(slot < 0, -1, slot + first)
        select = (number == code).astype(F32).astype(BF16)
        wide_ref[:, s * hid : (s + 1) * hid] = dot(select, act_refs[s][...]).astype(BF16)
    wide = out_refs[0].shape[1]
    for number, out_ref in enumerate(out_refs):
        for c in range(0, wide, 256):
            end = min(c + 256, wide)
            columns = slice(number * wide + c, number * wide + end)
            total = dot(wide_ref[:, :hid], w_refs[0][:, columns])
            for s in range(1, NY):
                total += dot(wide_ref[:, s * hid : (s + 1) * hid], w_refs[s][:, columns])
            for sent in sent_refs:
                total += sent[:, columns].astype(F32)
            out_ref[:, c:end] = total.astype(BF16)


def columns_of(rows, wide, at):
    return pl.BlockSpec((rows, wide), lambda i: (0, at))


def down_sums(block, choice, acts, weights, half, sent, tokens, seats):
    hid, part = weights[0].shape
    rows = NY * tokens
    wide, at = (part // 2, half) if half in (0, 1) else (part, 0)
    shape = jax.ShapeDtypeStruct((rows, part if half is None else part // 2), BF16)
    spec = pl.BlockSpec(memory_space=pltpu.VMEM)
    lanes = pl.BlockSpec((rows, LANES), lambda i: (0, part // LANES))
    columns = columns_of(hid, wide, at)
    there = [columns_of(rows, wide, at if r.shape[1] == part else 0) for r in sent]
    return pl.pallas_call(
        functools.partial(down_kernel, part, tokens, seats, len(sent)),
        out_shape=[shape] * (2 if half == 2 else 1),
        grid=(1,),
        in_specs=[lanes] + [spec] * (1 + NY) + [columns] * NY + there,
        out_specs=[spec] * (2 if half == 2 else 1),
        scratch_shapes=[pltpu.VMEM((rows, NY * hid), BF16)],
        compiler_params=pltpu.CompilerParams(vmem_limit_bytes=VMEM_BYTES),
        cost_estimate=LITTLE,
    )(block, choice, *acts, *weights, *sent)


def per_device(hidden, norm_gain, gate_weight, up_weight, down_weight, routes, logits):
    me = lax.axis_index("expert")
    odd = lax.axis_index("section") % 2
    y = jnp.where(odd == 1, (NY - me // NZ) % NY, me // NZ)
    tokens, width = hidden.shape[1], hidden.shape[2]
    top = routes.shape[2]
    hid = gate_weight.shape[2]
    part = width // NY
    experts = lax.axis_size("expert") // SLICES
    seats = 2 * tokens * top // experts
    gate, up, down = gate_weight[0], up_weight[0], down_weight[0]

    def place(d):
        return (y + d) % NY

    def gate_up_for(d, *earlier):
        at = after(place(d), *earlier) if earlier else place(d)
        start = (at * part, 0)
        return jnp.concatenate(
            [lax.dynamic_slice(w, start, (part, hid)) for w in (gate, up)], axis=1
        )

    def down_for(d, *earlier):
        return lax.dynamic_slice(down, (0, after(place(d), *earlier) * part), (hid, part))

    there_y = (NY - y) % NY
    places = (there_y + NY - jnp.arange(NY, dtype=jnp.int32)) % NY
    outgoing = quarters_of(hidden[0], places.astype(jnp.int32))
    rows = [next_section(r, (NY - s) % NY) for s, r in enumerate(outgoing)]
    lanes = route_lanes(*lax.optimization_barrier((routes[0], logits[0], rows[0]))[:2], experts)
    there = (jnp.arange(NY, dtype=jnp.int32) * jnp.where(odd == 1, -1, 1) + me // NZ) % NY
    choice = lane_choice(there * (NZ // SLICES) + me % NZ // SLICES, experts)
    homes = [lanes] + [moved(lanes, NY - s, 0) for s in range(1, NY)]
    gain = lax.dynamic_slice(norm_gain, (0, y * part), (1, part))
    block = normed_block(y, gain, rows, homes)
    arrived = next_section(hidden[0])

    x = {0: block}

    def step(k, forth, back):
        x[k] = moved(forth, 0, -1)
        if k < NZ // 2:
            x[-k] = moved(back, 0, 1)

    barrier = lax.optimization_barrier
    far, forth = barrier((gate_up_for(2, rows[0]), block))
    w_in = {2: moved(far, 2, 0)}
    step(1, forth, forth)
    step(2, x[1], x[-1])
    w_in[0], w_down = gate_up_for(0, x[1]), [down_for(0, x[1])]
    left, near, forth, back, w_in[2], arrived = barrier(
        (gate_up_for(3, x[1]), gate_up_for(1, x[1]), x[2], x[-2], w_in[2], arrived)
    )
    w_in[1], w_in[3] = moved(left, -1, 0), moved(near, 1, 0)
    step(3, forth, back)

    slots = NY * seats
    acts = {}

    def partials(keys, devices, *earlier):
        rows = [after(x[k], *earlier) for k in keys]
        return dict(zip(devices, hidden_partials(rows, choice, w_in, devices, tokens, seats)))

    def sent_out(sums, *earlier):
        return [sums[0]] + [moved(after(sums[s], *earlier), s, 0) for s in (1, 2, 3)]

    def activate(keys, sums, *earlier):
        total = after(sums[0], *earlier)
        for r in sums[1:]:
            total = total + r.astype(F32)
        act = (jax.nn.silu(total[:, :hid]) * total[:, hid:]).astype(BF16)
        everyone = [act] + [moved(act, -s, 0) for s in range(1, NY)]
        for i, k in enumerate(keys):
            acts[k] = (everyone, i)
        return act

    def down_of(k, half, sent, *earlier):
        group, at = acts[k]
        group = [after(group[0], *earlier)] + group[1:]
        block_acts = [a[at * slots : (at + 1) * slots] for a in group]
        sums = down_sums(x[k], choice, block_acts, w_down, half, sent, tokens, seats)
        return sums if half == 2 else sums[0]

    g4, g3, g2, g1 = (4,), (3, -3), (2, -2), (1, -1, 0)
    p1, p2 = (partials(g, (0, 2)) for g in (g1, g2))
    downs = [down_for(NY - s, x[2]) for s in (1, 2, 3)]
    forth, downs, w_in[1], w_in[3], *_ = barrier(
        (x[3], downs, w_in[1], w_in[3], p1[0], p2[0])
    )
    step(4, forth, None)
    w_down += [moved(w, -s, 0) for s, w in enumerate(downs, 1)]
    p3 = partials(g3, (2, 1, 3, 0))
    p2.update(partials(g2, (1, 3), p3[0]))
    p1.update(partials(g1, (1, 3), p2[1]))
    p4 = partials(g4, (2, 1, 3, 0), p1[1])
    h4 = [p4[0], moved(p4[1], 1, 0), moved(p4[2], 2, 0)]
    h4.append(moved(after(p4[3], *h4[1:], *w_down), 3, 0))
    activate(g4, h4)
    h3 = sent_out(p3, *acts[4][0][1:])
    s4 = down_of(4, None, [])
    plus = moved(s4, 0, 1)
    a3 = activate(g3, h3, s4)
    h2 = sent_out(p2, a3)
    r3 = down_of(-3, None, [])
    minus = moved(r3, 0, -1)
    s3 = down_of(3, None, [plus], r3)
    plus = moved(s3, 0, 1)
    a2 = activate(g2, h2, s3)
    h1 = sent_out(p1, a2)
    s2, r2 = down_of(2, None, [plus]), down_of(-2, None, [minus])
    plus, minus = moved(s2, 0, 1), moved(r2, 0, -1)
    activate(g1, h1, s2, r2)
    plus = [moved(s, 0, 1) for s in down_of(1, 2, [plus])]
    minus = [moved(s, 0, -1) for s in down_of(-1, 2, [minus])]
    halves = [down_of(0, c, [plus[c], minus[c]]) for c in (0, 1)]

    def gathered(home):
        def rows_for(d):
            return lax.dynamic_index_in_dim(home, place(d), 0, keepdims=False)

        there = [rows_for(0)] + [moved(rows_for(NY - s), -s, 0) for s in range(1, NY)]
        return jnp.roll(jnp.stack(there), y, axis=0)

    routed = [gathered(h.reshape(NY, tokens, part // 2)) for h in halves]
    routed = jnp.concatenate(routed, axis=2).transpose(1, 0, 2).reshape(tokens, width)
    mixed = (arrived.astype(F32) + routed.astype(F32)).astype(BF16)
    return mixed[None]


def solution(mesh):
    in_specs = (
        P("section", "expert", None),
        P("section", None),
        P("section", None, "expert"),
        P("section", None, "expert"),
        P("section", "expert", None),
        P("section", "expert", None),
        P("section", "expert", None),
    )
    out_specs = P("section", "expert", None)
    return jax.shard_map(
        per_device, mesh=mesh, in_specs=in_specs, out_specs=out_specs, check_vma=False
    )
```

```python
import functools

import jax
import jax.numpy as jnp
from jax import lax
from jax.experimental import pallas as pl
from jax.experimental.pallas import tpu as pltpu
from jax.sharding import PartitionSpec as P

ROUTE_SCALE = 2.5
EPSILON = 1e-06
NY = 4
NZ = 8
SLICES = 4
LANES = 128
BF16 = jnp.bfloat16
F32 = jnp.float32
VMEM_BYTES = 48 * 1024 * 1024
LITTLE = pl.CostEstimate(flops=1024, bytes_accessed=1024, transcendentals=0)


def moved(x, dy, dz):
    sections = lax.axis_size("section")
    pairs = []
    for s in range(sections):
        sign = 1 if s % 2 == 0 else -1
        for y in range(NY):
            for z in range(NZ):
                to = ((y + sign * dy) % NY) * NZ + (z + sign * dz) % NZ
                pairs.append((s * NY * NZ + y * NZ + z, s * NY * NZ + to))
    return lax.ppermute(x, ("section", "expert"), pairs)


def next_section(x, dy=0):
    sections = lax.axis_size("section")
    pairs = []
    for s in range(sections):
        to_section = (s + 1) % sections
        sign = 1 if to_section % 2 == 0 else -1
        for y in range(NY):
            for z in range(NZ):
                to = ((y + sign * dy) % NY) * NZ + z
                pairs.append((s * NY * NZ + y * NZ + z, to_section * NY * NZ + to))
    return lax.ppermute(x, ("section", "expert"), pairs)


def three_parts(x):
    high = lax.reduce_precision(x, 8, 7)
    middle = lax.reduce_precision(x - high, 8, 7)
    return [high, middle, x - high - middle]


def route_weights(scores):
    gate_values = jax.nn.sigmoid(scores)
    return ROUTE_SCALE * gate_values / jnp.sum(gate_values, axis=-1, keepdims=True)


def dot(a, b):
    return jnp.dot(a, b, preferred_element_type=F32)


def after(x, *others):
    return lax.optimization_barrier((x, *others))[0]


def route_lanes(routes, logits, experts):
    hits = routes[:, :, None] == jnp.arange(experts, dtype=jnp.int32)
    weight = jnp.sum(hits.astype(F32) * route_weights(logits)[:, :, None], axis=1)
    named = jnp.sum(hits.astype(jnp.int32), axis=1)
    slot = jnp.where(named > 0, jnp.cumsum(named, axis=0) - 1, -1).astype(F32)
    parts = jnp.concatenate(three_parts(weight) + [slot], axis=1).astype(BF16)
    return jnp.pad(parts, ((0, 0), (0, LANES - parts.shape[1])))


def lane_choice(columns, experts):
    lane = jnp.arange(LANES, dtype=jnp.int32)[None, :]
    expert = columns[:, None]
    weight = (lane == expert) | (lane == experts + expert) | (lane == 2 * experts + expert)
    slot = lane == 3 * experts + expert
    rows = jnp.concatenate([weight, slot], axis=0).astype(BF16)
    return jnp.pad(rows, ((0, LANES - rows.shape[0]), (0, 0)))


def quarter_kernel(place_ref, x_ref, *out_refs):
    tokens, width = x_ref.shape
    part = width // NY
    widened = x_ref[...].astype(F32)
    mean = jnp.sum(widened * widened, axis=-1, keepdims=True) * (1.0 / width)
    factor = lax.rsqrt(mean + EPSILON)
    high = factor.astype(BF16).astype(F32)
    middle = (factor - high).astype(BF16).astype(F32)
    low = factor - high - middle
    lane = lax.broadcasted_iota(jnp.int32, (tokens, LANES), 1)
    lanes = jnp.where(lane == 0, high, jnp.where(lane == 1, middle, jnp.where(lane == 2, low, 0.0)))
    for s, out_ref in enumerate(out_refs):
        first = pl.multiple_of(place_ref[s] * part, LANES)
        out_ref[:, :part] = x_ref[:, pl.ds(first, part)]
        out_ref[:, part:] = lanes.astype(BF16)


def quarters_of(rows, places):
    tokens, width = rows.shape
    spec = pl.BlockSpec(memory_space=pltpu.VMEM)
    shape = jax.ShapeDtypeStruct((tokens, width // NY + LANES), BF16)
    return pl.pallas_call(
        quarter_kernel,
        out_shape=[shape] * NY,
        in_specs=[pl.BlockSpec(memory_space=pltpu.SMEM), spec],
        out_specs=[spec] * NY,
        compiler_params=pltpu.CompilerParams(vmem_limit_bytes=VMEM_BYTES),
        cost_estimate=LITTLE,
    )(places, rows)


def block_kernel(part, y_ref, gain_ref, *refs):
    out_ref = refs[-1]
    tokens = refs[0].shape[0]
    for s in range(NY):
        row_ref, lane_ref = refs[s], refs[NY + s]
        home = pl.multiple_of(lax.rem(y_ref[0] + s, NY) * tokens, tokens)
        factor = row_ref[:, part:].astype(F32)
        factor = factor[:, :1] + factor[:, 1:2] + factor[:, 2:3]
        rows = row_ref[:, :part].astype(F32) * factor * gain_ref[...]
        out_ref[pl.ds(home, tokens), :part] = rows.astype(BF16)
        out_ref[pl.ds(home, tokens), part:] = lane_ref[...]


def normed_block(y, gain, rows, lanes):
    tokens, columns = rows[0].shape
    spec = pl.BlockSpec(memory_space=pltpu.VMEM)
    return pl.pallas_call(
        functools.partial(block_kernel, columns - LANES),
        out_shape=jax.ShapeDtypeStruct((NY * tokens, columns), BF16),
        in_specs=[pl.BlockSpec(memory_space=pltpu.SMEM)] + [spec] * (1 + 2 * NY),
        out_specs=spec,
        compiler_params=pltpu.CompilerParams(vmem_limit_bytes=VMEM_BYTES),
        cost_estimate=LITTLE,
    )(y.reshape(1).astype(jnp.int32), gain, *rows, *lanes)


def hidden_kernel(blocks, part, tokens, seats, devices, *refs):
    x_refs, choice_ref = refs[:blocks], refs[blocks]
    count = len(devices)
    w_refs = refs[blocks + 1 : blocks + 1 + count]
    out_refs = refs[blocks + 1 + count : blocks + 1 + 2 * count]
    picked_ref = refs[-1]
    rows = NY * tokens
    slots = NY * seats
    hid = w_refs[0].shape[1] // 2
    choice = choice_ref[...]
    number = lax.broadcasted_iota(jnp.int32, (slots, rows), 0)
    first = lax.broadcasted_iota(jnp.int32, (1, rows), 1) // tokens * seats
    for s, w_ref, out_ref in zip(devices, w_refs, out_refs):
        for b in range(blocks):
            info = lax.dot_general(
                choice,
                x_refs[b][:, part:],
                (((1,), (1,)), ((), ())),
                preferred_element_type=F32,
            )
            slot = info[NY + s : NY + s + 1, :].astype(jnp.int32)
            code = jnp.where(slot < 0, -1, slot + first)
            select = (number == code).astype(F32).astype(BF16)
            picked_ref[b * slots : (b + 1) * slots, :] = dot(select, x_refs[b][...]).astype(BF16)
        info = lax.dot_general(
            picked_ref[:, part:], choice, (((1,), (1,)), ((), ())), preferred_element_type=F32
        )
        sums = dot(picked_ref[:, :part], w_ref[...])
        out_ref[:, :hid] = sums[:, :hid].astype(out_ref.dtype)
        out_ref[:, hid:] = (sums[:, hid:] * info[:, s : s + 1]).astype(out_ref.dtype)


def hidden_partials(rows, choice, weights, devices, tokens, seats):
    blocks = len(rows)
    part, hid2 = weights[devices[0]].shape
    slots = NY * seats
    spec = pl.BlockSpec(memory_space=pltpu.VMEM)
    shape = (blocks * slots, hid2)
    count = len(devices)
    return pl.pallas_call(
        functools.partial(hidden_kernel, blocks, part, tokens, seats, devices),
        out_shape=[jax.ShapeDtypeStruct(shape, F32 if s == 0 else BF16) for s in devices],
        in_specs=[spec] * (blocks + 1 + count),
        out_specs=[spec] * count,
        scratch_shapes=[pltpu.VMEM((blocks * slots, part + LANES), BF16)],
        compiler_params=pltpu.CompilerParams(vmem_limit_bytes=VMEM_BYTES),
        cost_estimate=LITTLE,
    )(*rows, choice, *[weights[s] for s in devices])


def down_kernel(part, tokens, seats, arriving, *refs):
    x_ref, choice_ref = refs[:2]
    act_refs = refs[2 : 2 + NY]
    w_refs = refs[2 + NY : 2 + 2 * NY]
    sent_refs = refs[2 + 2 * NY : 2 + 2 * NY + arriving]
    out_refs, wide_ref = refs[2 + 2 * NY + arriving : -1], refs[-1]
    rows = NY * tokens
    slots = NY * seats
    hid = act_refs[0].shape[1]
    info = lax.dot_general(
        x_ref[...], choice_ref[...], (((1,), (1,)), ((), ())), preferred_element_type=F32
    )
    number = lax.broadcasted_iota(jnp.int32, (rows, slots), 1)
    first = lax.broadcasted_iota(jnp.int32, (rows, 1), 0) // tokens * seats
    for s in range(NY):
        slot = info[:, NY + s : NY + s + 1].astype(jnp.int32)
        code = jnp.where(slot < 0, -1, slot + first)
        select = (number == code).astype(F32).astype(BF16)
        wide_ref[:, s * hid : (s + 1) * hid] = dot(select, act_refs[s][...]).astype(BF16)
    wide = out_refs[0].shape[1]
    for number, out_ref in enumerate(out_refs):
        for c in range(0, wide, 256):
            end = min(c + 256, wide)
            columns = slice(number * wide + c, number * wide + end)
            total = dot(wide_ref[:, :hid], w_refs[0][:, columns])
            for s in range(1, NY):
                total += dot(wide_ref[:, s * hid : (s + 1) * hid], w_refs[s][:, columns])
            for sent in sent_refs:
                total += sent[:, columns].astype(F32)
            out_ref[:, c:end] = total.astype(BF16)


def columns_of(rows, wide, at):
    return pl.BlockSpec((rows, wide), lambda i: (0, at))


def down_sums(block, choice, acts, weights, half, sent, tokens, seats):
    hid, part = weights[0].shape
    rows = NY * tokens
    wide, at = (part // 2, half) if half in (0, 1) else (part, 0)
    shape = jax.ShapeDtypeStruct((rows, part if half is None else part // 2), BF16)
    spec = pl.BlockSpec(memory_space=pltpu.VMEM)
    lanes = pl.BlockSpec((rows, LANES), lambda i: (0, part // LANES))
    columns = columns_of(hid, wide, at)
    there = [columns_of(rows, wide, at if r.shape[1] == part else 0) for r in sent]
    return pl.pallas_call(
        functools.partial(down_kernel, part, tokens, seats, len(sent)),
        out_shape=[shape] * (2 if half == 2 else 1),
        grid=(1,),
        in_specs=[lanes] + [spec] * (1 + NY) + [columns] * NY + there,
        out_specs=[spec] * (2 if half == 2 else 1),
        scratch_shapes=[pltpu.VMEM((rows, NY * hid), BF16)],
        compiler_params=pltpu.CompilerParams(vmem_limit_bytes=VMEM_BYTES),
        cost_estimate=LITTLE,
    )(block, choice, *acts, *weights, *sent)


def per_device(hidden, norm_gain, gate_weight, up_weight, down_weight, routes, logits):
    me = lax.axis_index("expert")
    odd = lax.axis_index("section") % 2
    y = jnp.where(odd == 1, (NY - me // NZ) % NY, me // NZ)
    tokens, width = hidden.shape[1], hidden.shape[2]
    top = routes.shape[2]
    hid = gate_weight.shape[2]
    part = width // NY
    experts = lax.axis_size("expert") // SLICES
    seats = 2 * tokens * top // experts
    gate, up, down = gate_weight[0], up_weight[0], down_weight[0]

    def place(d):
        return (y + d) % NY

    def gate_up_for(d, *earlier):
        at = after(place(d), *earlier) if earlier else place(d)
        start = (at * part, 0)
        return jnp.concatenate(
            [lax.dynamic_slice(w, start, (part, hid)) for w in (gate, up)], axis=1
        )

    def down_for(d, *earlier):
        return lax.dynamic_slice(down, (0, after(place(d), *earlier) * part), (hid, part))

    there_y = (NY - y) % NY
    places = (there_y + NY - jnp.arange(NY, dtype=jnp.int32)) % NY
    outgoing = quarters_of(hidden[0], places.astype(jnp.int32))
    rows = [next_section(r, (NY - s) % NY) for s, r in enumerate(outgoing)]
    lanes = route_lanes(*lax.optimization_barrier((routes[0], logits[0], rows[0]))[:2], experts)
    there = (jnp.arange(NY, dtype=jnp.int32) * jnp.where(odd == 1, -1, 1) + me // NZ) % NY
    choice = lane_choice(there * (NZ // SLICES) + me % NZ // SLICES, experts)
    homes = [lanes] + [moved(lanes, NY - s, 0) for s in range(1, NY)]
    gain = lax.dynamic_slice(norm_gain, (0, y * part), (1, part))
    block = normed_block(y, gain, rows, homes)
    arrived = next_section(hidden[0])

    x = {0: block}

    def step(k, forth, back):
        x[k] = moved(forth, 0, -1)
        if k < NZ // 2:
            x[-k] = moved(back, 0, 1)

    barrier = lax.optimization_barrier
    far, forth = barrier((gate_up_for(2, rows[0]), block))
    w_in = {2: moved(far, 2, 0)}
    step(1, forth, forth)
    step(2, x[1], x[-1])
    w_in[0], w_down = gate_up_for(0, x[1]), [down_for(0, x[1])]
    left, near, forth, back, w_in[2], arrived = barrier(
        (gate_up_for(3, x[1]), gate_up_for(1, x[1]), x[2], x[-2], w_in[2], arrived)
    )
    w_in[1], w_in[3] = moved(left, -1, 0), moved(near, 1, 0)
    step(3, forth, back)

    slots = NY * seats
    acts = {}

    def partials(keys, devices, *earlier):
        rows = [after(x[k], *earlier) for k in keys]
        return dict(zip(devices, hidden_partials(rows, choice, w_in, devices, tokens, seats)))

    def sent_out(sums, *earlier):
        return [sums[0]] + [moved(after(sums[s], *earlier), s, 0) for s in (1, 2, 3)]

    def activate(keys, sums, *earlier):
        total = after(sums[0], *earlier)
        for r in sums[1:]:
            total = total + r.astype(F32)
        act = (jax.nn.silu(total[:, :hid]) * total[:, hid:]).astype(BF16)
        everyone = [act] + [moved(act, -s, 0) for s in range(1, NY)]
        for i, k in enumerate(keys):
            acts[k] = (everyone, i)
        return act

    def down_of(k, half, sent, *earlier):
        group, at = acts[k]
        group = [after(group[0], *earlier)] + group[1:]
        block_acts = [a[at * slots : (at + 1) * slots] for a in group]
        sums = down_sums(x[k], choice, block_acts, w_down, half, sent, tokens, seats)
        return sums if half == 2 else sums[0]

    g4, g3, g2, g1 = (4,), (3, -3), (2, -2), (1, -1, 0)
    p1, p2 = (partials(g, (0, 2)) for g in (g1, g2))
    downs = [down_for(NY - s, x[2]) for s in (1, 2, 3)]
    forth, downs, w_in[1], w_in[3], *_ = barrier(
        (x[3], downs, w_in[1], w_in[3], p1[0], p2[0])
    )
    step(4, forth, None)
    w_down += [moved(w, -s, 0) for s, w in enumerate(downs, 1)]
    p3 = partials(g3, (2, 1, 3, 0))
    p2.update(partials(g2, (1, 3), p3[0]))
    p1.update(partials(g1, (1, 3), p2[1]))
    p4 = partials(g4, (2, 1, 3, 0), p1[1])
    h4 = sent_out(p4, *w_down)
    activate(g4, h4)
    h3 = sent_out(p3, *acts[4][0][1:])
    s4 = down_of(4, None, [])
    plus = moved(s4, 0, 1)
    a3 = activate(g3, h3, s4)
    h2 = sent_out(p2, a3)
    r3 = down_of(-3, None, [])
    minus = moved(r3, 0, -1)
    s3 = down_of(3, None, [plus], r3)
    plus = moved(s3, 0, 1)
    a2 = activate(g2, h2, s3)
    h1 = sent_out(p1, a2)
    s2, r2 = down_of(2, None, [plus]), down_of(-2, None, [minus])
    plus, minus = moved(s2, 0, 1), moved(r2, 0, -1)
    activate(g1, h1, s2, r2)
    s1 = down_of(1, 2, [plus])
    r1 = down_of(-1, 2, [minus], s1[0])
    plus, minus = [moved(s, 0, 1) for s in s1], [moved(s, 0, -1) for s in r1]
    halves = [down_of(0, c, [plus[c], minus[c]]) for c in (0, 1)]

    def gathered(home):
        def rows_for(d):
            return lax.dynamic_index_in_dim(home, place(d), 0, keepdims=False)

        there = [rows_for(0)] + [moved(rows_for(NY - s), -s, 0) for s in range(1, NY)]
        return jnp.roll(jnp.stack(there), y, axis=0)

    routed = [gathered(h.reshape(NY, tokens, part // 2)) for h in halves]
    routed = jnp.concatenate(routed, axis=2).transpose(1, 0, 2).reshape(tokens, width)
    mixed = (arrived.astype(F32) + routed.astype(F32)).astype(BF16)
    return mixed[None]


def solution(mesh):
    in_specs = (
        P("section", "expert", None),
        P("section", None),
        P("section", None, "expert"),
        P("section", None, "expert"),
        P("section", "expert", None),
        P("section", "expert", None),
        P("section", "expert", None),
    )
    out_specs = P("section", "expert", None)
    return jax.shard_map(
        per_device, mesh=mesh, in_specs=in_specs, out_specs=out_specs, check_vma=False
    )
```
